256 devices in a mesh: pos: 32 (over x, z), ch: 8 (over y, core).
Axes of the slice: x: 4, y: 4, z: 8, core: 2. Of those that a mesh axis runs over, the one named last changes fastest.
Arguments:
- track_grad: bfloat16 [768, 262144], P('ch', 'pos'), may hold values from -6 to 6
- activation: bfloat16 [768, 262144], P('ch', 'pos'), may hold values from -6 to 6
- coarse_in: bfloat16 [768, 131072], P('ch', 'pos'), may hold values from -6 to 6
- tap_weight: bfloat16 [4, 768, 768], P(None, 'ch'), may hold values from -0.15625 to 0.15625
- score_grad: float32 [65536], P('pos'), may hold values from -96 to 96
- donor_row: int32 [65536], P('pos'), may hold values from 0 to 8191
- acceptor_owner: int32 [65536, 1], P('pos'), may hold values from 0 to 31; in each aligned block of 2048 rows (0 to 2047, 2048 to 4095, ...) at most 256 rows name the same one
- acceptor_row: int32 [65536], P('pos'), may hold values from 0 to 8191
Outputs:
- skip_grad: bfloat16 [768, 262144], P('ch', 'pos')
- coarse_grad: bfloat16 [768, 131072], P('ch', 'pos')
- weight_grad: bfloat16 [4, 768, 768], P(None, 'ch', 'pos')
The draws below stay inside these ranges and needn't reach their ends.
Inputs may be any that keep to these rules, and one draw needn't show every extreme that they name: `acceptor_owner`: within the 2048 rows of one index of pos, no value appears more than 256 times; some value appears exactly 256 times.
All inputs are finite; a program needn't handle non-finite values.
Results may differ from the reference program's by a relative error of at most 0.0043.
Values may be sent and summed in bfloat16 or wider, within the bound.
A program may use at most 128 MiB of HBM per device.

```python
import math
import jax
import jax.numpy as jnp
import numpy as np
from jax import lax

C = 768
KERNEL = 4
T_DEV = 8192
J_DEV = 2048
LENGTH = 262144
COARSE = 131072
JUNCS = 65536
CAP = 256
N_POS = 32


def set_ends(array, stream_key, low, high):
    longest = array.shape.index(max(array.shape))
    spots = []
    for shift in (0, 1):
        where = [jax.random.randint(jax.random.fold_in(stream_key, axis), (), 0, length) for axis, length in enumerate(array.shape)]
        where[longest] = (where[longest] + shift) % array.shape[longest]
        spots.append(tuple(where))
    return array.at[spots[0]].set(low).at[spots[1]].set(high)


def with_spikes(values, key, source, target, parts, factor):
    def block_of(dim):
        return (jnp.arange(values.shape[dim]) // (values.shape[dim] // parts)).reshape((-1,) + (1,) * (values.ndim - 1 - dim))

    first = jax.random.permutation(key, parts)[block_of(target)]
    other_side = (block_of(target) + parts // 2) % parts
    return jnp.where((block_of(source) == first) | (block_of(source) == other_side), factor * values, values)


def block_levels(own_key, shape, shards, least, high):
    gain = 1.0
    for axis_at, shards_of in shards:
        draws = jax.random.uniform(jax.random.fold_in(jax.random.fold_in(own_key, 6), axis_at), (shards_of,), jnp.float32, least / len(shards), high / len(shards))
        gain = gain * jnp.repeat(jnp.exp(draws), shape[axis_at] // shards_of).reshape((-1,) + (1,) * (len(shape) - 1 - axis_at))
    return gain


def assign_block(key, own, number, rows, amount, top, limit, slope):
    order = jax.random.permutation(key, amount)
    heavy_load, usual = load_shares(amount, rows * top, limit, slope, True), load_shares(amount, rows * top, limit, slope, False)
    places = jnp.arange(amount)

    def named(sizes, turn):
        used = int((sizes > 0).sum())
        fixed = max(1, used // 4)
        moved = fixed + (places - fixed + turn * (used - fixed)) % max(1, amount - fixed)
        return jnp.zeros((amount,), jnp.int32).at[order[jnp.where(places < fixed, places, moved)]].set(jnp.asarray(sizes, jnp.int32))

    sizes = jnp.where(number % 4 == 0, named(heavy_load, number // 4), named(usual, number - number // 4 - 1))
    mixed = jax.random.permutation(jax.random.fold_in(own, 3), amount)
    donor, receiver = mixed[0:amount // 2 * 2:2], mixed[1:amount // 2 * 2:2]
    margin = jnp.minimum(sizes[donor] - 1, limit - sizes[receiver]) // 2
    margin = jnp.where((donor == order[0]) | (receiver == order[0]) | (sizes[receiver] == 0), 0, jnp.maximum(margin, 0))
    moved = jax.random.randint(jax.random.fold_in(own, 4), (amount // 2,), 0, 1 << 20) % (margin + 1)
    sizes = sizes.at[donor].add(-moved).at[receiver].add(moved)
    items = jnp.searchsorted(jnp.cumsum(sizes), jnp.arange(rows * top), side="right").astype(jnp.int32)
    table = items.reshape(top, rows).T
    table = table[jax.random.permutation(jax.random.fold_in(own, 1), rows)]
    turn = jax.random.randint(jax.random.fold_in(own, 2), (rows, 1), 0, top)
    return jnp.take_along_axis(table, (jnp.arange(top)[None, :] + turn) % top, axis=1)


def load_shares(number_of, total, bound, lean, full):
    portions = [(1 << 20) // math.isqrt(standing ** lean) + 1 for standing in range(1, number_of + 1)]
    largest = bound if full else min(bound, max(-(-total // number_of), total * portions[0] // sum(portions)))
    least = 1 if total - largest >= number_of - 1 else 0
    holding, spare = [largest] + [least] * (number_of - 1), total - largest - least * (number_of - 1)
    while spare > 0:
        movable = [i for i in range(1, number_of) if holding[i] < largest] or [i for i in range(1, number_of) if holding[i] < bound]
        whole, remaining = sum([portions[i] for i in movable]), spare
        for i in movable:
            extra = min(bound - holding[i], max(1, remaining * portions[i] // whole), spare)
            holding[i] = holding[i] + extra
            spare = spare - extra
    return np.array(holding)


def gaussian(key, dims, spread, limit, cuts=(), held_as=jnp.bfloat16):
    result = jax.random.normal(key, dims, jnp.float32) * spread
    if len(cuts) > 0:
        result = block_levels(key, dims, cuts, -0.22, 0.18) * result
    return jnp.clip(result, min=-limit, max=limit).astype(held_as)


def heavy_noise(rng, shape, width, bound, pieces, heavy, held_as=jnp.bfloat16):
    values = width * jax.random.normal(rng, shape, jnp.float32)
    if pieces:
        values = values * block_levels(rng, shape, pieces, -0.22, 0.18)
    return jnp.clip(with_spikes(values, jax.random.fold_in(rng, 3), *heavy), -bound, bound).astype(held_as)


def setup_inputs(seed: int = 0) -> dict:
    arg_keys = jax.random.split(jax.random.key(seed), 9)
    track_grad = gaussian(arg_keys[0], (C, LENGTH), 1.0, 6.0, ((0, 8), (1, 32)))
    activation = gaussian(arg_keys[1], (C, LENGTH), 1.0, 6.0, ((0, 8), (1, 32)))
    coarse_in = heavy_noise(arg_keys[2], (C, COARSE), 1.0, 6.0, ((0, 8), (1, 32)), (1, 0, 32, 2.75))
    tap_weight = gaussian(arg_keys[3], (KERNEL, C, C), (2 * C) ** -0.5, 0.15625, ((1, 8),))
    score_grad = gaussian(arg_keys[4], (JUNCS,), 16.0, 96.0, ((0, 32),), jnp.float32)
    donor_row = set_ends(jax.random.randint(arg_keys[5], (JUNCS,), 0, T_DEV), jax.random.fold_in(arg_keys[5], 1), 0, T_DEV - 1).astype(jnp.int32)
    acceptor_owner_keys = jax.random.split(jax.random.fold_in(arg_keys[6], 1), JUNCS // J_DEV)
    acceptor_owner_turns = jax.random.permutation(jax.random.fold_in(arg_keys[6], 3), JUNCS // J_DEV)
    acceptor_owner = jax.vmap(lambda own, number: assign_block(jax.random.fold_in(arg_keys[6], 2), own, number, J_DEV, N_POS, 1, CAP, 2))(acceptor_owner_keys, acceptor_owner_turns).reshape((JUNCS, 1))
    acceptor_row = set_ends(jax.random.randint(arg_keys[7], (JUNCS,), 0, T_DEV), jax.random.fold_in(arg_keys[7], 1), 0, T_DEV - 1).astype(jnp.int32)
    return {"track_grad": track_grad, "activation": activation, "coarse_in": coarse_in, "tap_weight": tap_weight, "score_grad": score_grad, "donor_row": donor_row, "acceptor_owner": acceptor_owner, "acceptor_row": acceptor_row}


def reference(track_grad, activation, coarse_in, tap_weight, score_grad, donor_row, acceptor_owner, acceptor_row):
    holders = jnp.arange(JUNCS, dtype=jnp.int32) // J_DEV
    donor_pos = (holders * T_DEV + donor_row).astype(jnp.int32)
    acceptor_pos = (acceptor_owner[:, 0] * T_DEV + acceptor_row).astype(jnp.int32)
    factor = score_grad * (1.0 / math.sqrt(C))
    donor_vals = jnp.take(activation, donor_pos, axis=1).astype(jnp.float32)
    acceptor_vals = jnp.take(activation, acceptor_pos, axis=1).astype(jnp.float32)
    acceptor_terms = lax.optimization_barrier((donor_vals * factor[None, :]).astype(jnp.bfloat16))
    running = track_grad.astype(jnp.float32)
    running = running.at[:, donor_pos].add(acceptor_vals * factor[None, :])
    running = running.at[:, acceptor_pos].add(acceptor_terms.astype(jnp.float32))
    skip_grad = running.astype(jnp.bfloat16)
    extended = jnp.pad(skip_grad, ((0, 0), (1, 1)))
    coarse_acc = jnp.zeros((C, COARSE), jnp.float32)
    weight_list = []
    for offset in range(KERNEL):
        shifted = extended[:, offset:offset + LENGTH:2]
        coarse_acc = coarse_acc + jnp.dot(tap_weight[offset].T, shifted, preferred_element_type=jnp.float32)
        weight_list.append(jnp.dot(shifted, coarse_in.T, preferred_element_type=jnp.float32))
    weight_grad = (jnp.stack(weight_list) * (1.0 / math.sqrt(COARSE))).astype(jnp.bfloat16)
    return (skip_grad, coarse_acc.astype(jnp.bfloat16), weight_grad)
```

```python
import functools
import math

import jax
import jax.numpy as jnp
from jax import lax
from jax.experimental import pallas as pl
from jax.experimental.pallas import tpu as pltpu
from jax.sharding import PartitionSpec as P

C = 768
KERNEL = 4
BF = jnp.bfloat16
F32 = jnp.float32
MESH = pl.DeviceIdType.MESH
NT = (((1,), (1,)), ((), ()))
PARTS = 4


def tail_kernel(
    peers, ring, chan, total,
    even_ref, odd_ref, wt_ref, full_hbm,
    coarse_ref, weight_ref,
    full, taps, halo_even, halo_odd, pair_out, pair_in, part, relay, before, after,
    weight_acc, weight_out, weight_in,
    full_sem, halo_send, halo_recv, pair_send, pair_recv, relay_send, relay_recv,
    direct_send, direct_recv, sum_send, sum_recv, weight_send, weight_recv,
):
    me = lax.axis_index("pos")
    ch = lax.axis_index("ch")
    core = lax.rem(ch, 2)
    row = ch // 2
    sibling = ch + 1 - 2 * core
    up = lax.rem(ch + 2, 2 * ring)
    down = lax.rem(ch + 2 * ring - 2, 2 * ring)
    row_up, row_down = lax.rem(row + 1, ring), lax.rem(row + ring - 1, ring)
    row_far = lax.rem(row + 2, ring)
    wide = even_ref.shape[1]
    piece = wide // PARTS
    rows_in = weight_ref.shape[0]
    pos_up, pos_down = lax.rem(me + 1, peers), lax.rem(me + peers - 1, peers)

    load_full = pltpu.make_async_copy(full_hbm, full, full_sem)
    load_full.start()

    barrier = pltpu.get_barrier_semaphore()

    def greet(off, carry):
        pl.semaphore_signal(barrier, inc=1, device_id={"pos": lax.rem(me + off, peers)}, device_id_type=MESH)
        return carry

    lax.fori_loop(1, peers, greet, 0)
    for other in (sibling, up, down):
        pl.semaphore_signal(barrier, inc=1, device_id={"ch": other}, device_id_type=MESH)
    pl.semaphore_wait(barrier, peers + 2)

    edge = halo_even.shape[1]
    to_up = pltpu.make_async_remote_copy(
        odd_ref.at[:, pl.ds(wide - edge, edge)], halo_odd, halo_send.at[0], halo_recv.at[0],
        device_id={"pos": pos_up}, device_id_type=MESH)
    to_down = pltpu.make_async_remote_copy(
        even_ref.at[:, pl.ds(0, edge)], halo_even, halo_send.at[1], halo_recv.at[1],
        device_id={"pos": pos_down}, device_id_type=MESH)
    to_up.start()
    to_down.start()
    taps[pl.ds(chan, chan), :] = even_ref[...]
    taps[pl.ds(2 * chan, chan), :] = odd_ref[...]
    spot = lax.broadcasted_iota(jnp.int32, (chan, wide), 1)
    moved_odd = pltpu.roll(odd_ref[...].astype(F32), 1, 1)
    moved_even = pltpu.roll(even_ref[...].astype(F32), wide - 1, 1)
    to_up.wait()
    to_down.wait()
    first = halo_odd[...].astype(F32)[:, edge - 1:edge] * jnp.where(me == 0, 0.0, 1.0)
    last = halo_even[...].astype(F32)[:, 0:1] * jnp.where(me == peers - 1, 0.0, 1.0)
    taps[pl.ds(0, chan), :] = jnp.where(spot == 0, first, moved_odd).astype(BF)
    taps[pl.ds(3 * chan, chan), :] = jnp.where(spot == wide - 1, last, moved_even).astype(BF)

    half = ring * chan

    def pair_copy(q):
        return pltpu.make_async_remote_copy(
            pair_out.at[q], pair_in.at[q], pair_send.at[q], pair_recv.at[q],
            device_id={"ch": sibling}, device_id_type=MESH)

    def relay_copy(q):
        return pltpu.make_async_remote_copy(
            part.at[q, row_far], relay.at[q], relay_send.at[q], relay_recv.at[q],
            device_id={"ch": up if q < PARTS // 2 else down}, device_id_type=MESH)

    def direct_copy(q):
        rising = q >= PARTS // 2
        return pltpu.make_async_remote_copy(
            part.at[q, row_up if rising else row_down], (before if rising else after).at[q],
            direct_send.at[q], direct_recv.at[q],
            device_id={"ch": up if rising else down}, device_id_type=MESH)

    def sum_copy(q):
        rising = q < PARTS // 2
        return pltpu.make_async_remote_copy(
            part.at[q, row_up if rising else row_down], (before if rising else after).at[q],
            sum_send.at[q], sum_recv.at[q],
            device_id={"ch": up if rising else down}, device_id_type=MESH)

    order = (0, PARTS // 2, 1, PARTS // 2 + 1)
    for q in order:
        block = taps[:, q * piece:(q + 1) * piece]
        pair_out[q] = jnp.dot(
            wt_ref[pl.ds((1 - core) * half, half), :], block, preferred_element_type=F32
        ).astype(BF).reshape(ring, chan, piece)
        pair_copy(q).start()
    for q in order:
        block = taps[:, q * piece:(q + 1) * piece]
        mine = jnp.dot(wt_ref[pl.ds(core * half, half), :], block, preferred_element_type=F32)
        pair_copy(q).wait_recv()
        both = mine.reshape(ring, chan, piece) + pair_in[q].astype(F32)
        part[q] = both.astype(BF)
        relay_copy(q).start()
    for q in order:
        direct_copy(q).start()

    load_full.wait()
    for q in range(PARTS):
        where = slice(q * piece, (q + 1) * piece)
        term = lax.dot_general(full[:, where], taps[:, where], NT, preferred_element_type=F32)
        if q == 0:
            weight_acc[...] = term
        else:
            weight_acc[...] += term
    kept = weight_out.shape[1]
    for p in range(peers):
        weight_out[p] = jnp.concatenate(
            [weight_acc[p * rows_in:(p + 1) * rows_in, :],
             jnp.zeros((kept - rows_in, weight_acc.shape[1]), F32)], axis=0).astype(BF)

    def weight_copy(off):
        other = lax.rem(me + off, peers)
        return pltpu.make_async_remote_copy(
            weight_out.at[other], weight_in.at[me], weight_send.at[other], weight_recv.at[me],
            device_id={"pos": other}, device_id_type=MESH)

    def weight_start(off, carry):
        weight_copy(off).start()
        return carry

    lax.fori_loop(1, peers, weight_start, 0)

    for q in order:
        rising = q < PARTS // 2
        relay_copy(q).wait_recv()
        goal = row_up if rising else row_down
        part[q, goal] = (part[q, goal].astype(F32) + relay[q].astype(F32)).astype(BF)
        sum_copy(q).start()
    for q in order:
        direct_copy(q).wait_recv()
        sum_copy(q).wait_recv()
        coarse_ref[:, q * piece:(q + 1) * piece] = (
            part[q, row].astype(F32) + before[q].astype(F32) + after[q].astype(F32)).astype(BF)

    own = weight_out[me]
    weight_acc[pl.ds(0, kept), :] = own.astype(F32)

    def weight_add(off, carry):
        source = lax.rem(me + peers - off, peers)
        pltpu.make_async_remote_copy(
            weight_out.at[source], weight_in.at[source], weight_send.at[source], weight_recv.at[source],
            device_id={"pos": source}, device_id_type=MESH).wait_recv()
        weight_acc[pl.ds(0, kept), :] += weight_in[source].astype(F32)
        return carry

    lax.fori_loop(1, peers, weight_add, 0)
    weight_ref[...] = weight_acc[0:rows_in, :] * (1.0 / math.sqrt(total))

    for q in order:
        pair_copy(q).wait_send()
        relay_copy(q).wait_send()
        direct_copy(q).wait_send()
        sum_copy(q).wait_send()

    def weight_sent(off, carry):
        weight_copy(off).wait_send()
        return carry

    lax.fori_loop(1, peers, weight_sent, 0)


def tail(even, odd, wt, full, peers, ring, chan, total):
    wide = even.shape[1]
    piece = wide // PARTS
    channels = full.shape[0]
    rows_in = channels // peers
    kept = -(-rows_in // 16) * 16
    outs = KERNEL * chan
    edge = min(128, wide)
    dma = pltpu.SemaphoreType.DMA
    vmem = pl.BlockSpec(memory_space=pltpu.VMEM)
    return pl.pallas_call(
        functools.partial(tail_kernel, peers, ring, chan, total),
        out_shape=(jax.ShapeDtypeStruct((chan, wide), BF), jax.ShapeDtypeStruct((rows_in, outs), F32)),
        in_specs=[vmem, vmem, vmem, pl.BlockSpec(memory_space=pl.ANY)],
        out_specs=(vmem, vmem),
        scratch_shapes=[
            pltpu.VMEM((channels, wide), BF),
            pltpu.VMEM((outs, wide), BF),
            pltpu.VMEM((chan, edge), BF),
            pltpu.VMEM((chan, edge), BF),
            pltpu.VMEM((PARTS, ring, chan, piece), BF),
            pltpu.VMEM((PARTS, ring, chan, piece), BF),
            pltpu.VMEM((PARTS, ring, chan, piece), BF),
            pltpu.VMEM((PARTS, chan, piece), BF),
            pltpu.VMEM((PARTS, chan, piece), BF),
            pltpu.VMEM((PARTS, chan, piece), BF),
            pltpu.VMEM((channels, outs), F32),
            pltpu.VMEM((peers, kept, outs), BF),
            pltpu.VMEM((peers, kept, outs), BF),
            dma, dma((2,)), dma((2,)), dma((PARTS,)), dma((PARTS,)), dma((PARTS,)), dma((PARTS,)),
            dma((PARTS,)), dma((PARTS,)), dma((PARTS,)), dma((PARTS,)), dma((peers,)), dma((peers,)),
        ],
        compiler_params=pltpu.CompilerParams(
            collective_id=1, has_side_effects=True, vmem_limit_bytes=56 * 1024 * 1024),
        cost_estimate=pl.CostEstimate(flops=4 * channels * outs * wide, bytes_accessed=2 * channels * wide * 2, transcendentals=0),
        name="tail",
    )(even, odd, wt, full)


def split_weight(tap_weight, ring, chan):
    taps, chan_local, channels = tap_weight.shape
    table = tap_weight.reshape(taps * chan_local, ring, 2, chan)
    return table.transpose(2, 1, 3, 0).reshape(channels, taps * chan_local)


def shards(
    track_grad,
    activation,
    coarse_in,
    tap_weight,
    score_grad,
    donor_row,
    acceptor_owner,
    acceptor_row,
):
    ring = lax.axis_size("ch") // 2
    full_in = lax.all_gather(coarse_in, "ch", axis=0, tiled=True)
    wt = split_weight(tap_weight, ring, track_grad.shape[0])
    chan_local, local_len = track_grad.shape
    junc_count = score_grad.shape[0]
    pos_count = lax.axis_size("pos")
    capacity = junc_count // 8
    factor = score_grad * (1.0 / math.sqrt(C))
    owners = acceptor_owner[:, 0]
    members = (owners[:, None] == jnp.arange(pos_count, dtype=jnp.int32)[None, :]).astype(jnp.int32)
    rank_list = jnp.cumsum(members, axis=0) - 1
    within = jnp.sum(rank_list * members, axis=1)
    flat_slot = owners * capacity + within
    request_rows = (
        jnp.zeros((pos_count * capacity,), jnp.int32)
        .at[flat_slot]
        .set(acceptor_row)
        .reshape(1, pos_count, capacity)
    )
    donor_vals = jnp.take(activation, donor_row, axis=1).astype(jnp.float32)
    acceptor_terms = (donor_vals * factor[None, :]).astype(jnp.bfloat16)
    term_buffer = (
        jnp.zeros((chan_local, pos_count * capacity), jnp.bfloat16)
        .at[:, flat_slot]
        .set(acceptor_terms)
        .reshape(chan_local, pos_count, capacity)
    )
    got_rows = lax.all_to_all(request_rows, "pos", split_axis=1, concat_axis=1, tiled=True)
    fetched = jnp.take(activation, got_rows[0], axis=1)
    returned = lax.all_to_all(fetched, "pos", split_axis=1, concat_axis=1, tiled=True)
    got_terms = lax.all_to_all(term_buffer, "pos", split_axis=1, concat_axis=1, tiled=True)
    acceptor_vals = returned[:, owners, within].astype(jnp.float32)
    running = track_grad.astype(jnp.float32)
    running = running.at[:, donor_row].add(acceptor_vals * factor[None, :])
    running = running.at[:, got_rows.reshape(-1)].add(
        got_terms.reshape(chan_local, -1).astype(jnp.float32)
    )
    skip_grad = running.astype(jnp.bfloat16)
    order = jnp.arange(256)
    place = jnp.where(order % 2 == 0, order // 2, 128 + order // 2)
    pick = (place[:, None] == order[None, :]).astype(BF)
    split = jnp.einsum(
        "cbt,tu->cbu", skip_grad.reshape(chan_local, local_len // 256, 256), pick, preferred_element_type=F32
    ).astype(BF)
    even = split[:, :, :128].reshape(chan_local, local_len // 2)
    odd = split[:, :, 128:].reshape(chan_local, local_len // 2)
    coarse_grad, weight_rows = tail(
        even, odd, wt, full_in, pos_count, ring, chan_local, coarse_in.shape[1] * pos_count
    )
    weight_grad = weight_rows.reshape(-1, KERNEL, chan_local).transpose(1, 2, 0).astype(BF)
    return (skip_grad, coarse_grad, weight_grad)

def solution(mesh):
    in_specs = (
        P("ch", "pos"),
        P("ch", "pos"),
        P("ch", "pos"),
        P(None, "ch", None),
        P("pos"),
        P("pos"),
        P("pos", None),
        P("pos"),
    )
    out_specs = (P("ch", "pos"), P("ch", "pos"), P(None, "ch", "pos"))
    return jax.shard_map(shards, mesh=mesh, in_specs=in_specs, out_specs=out_specs, check_vma=False)
```

```python
import functools
import math

import jax
import jax.numpy as jnp
from jax import lax
from jax.experimental import pallas as pl
from jax.experimental.pallas import tpu as pltpu
from jax.sharding import PartitionSpec as P

C = 768
KERNEL = 4
BF = jnp.bfloat16
F32 = jnp.float32
MESH = pl.DeviceIdType.MESH
NT = (((1,), (1,)), ((), ()))
PARTS = 4


def tail_kernel(
    peers, ring, chan, total,
    even_ref, odd_ref, wt_ref, full_hbm,
    coarse_ref, weight_ref,
    full, taps, halo_even, halo_odd, pair_out, pair_in, part, exact, relay, before, after,
    weight_acc, weight_out, weight_in,
    full_sem, halo_send, halo_recv, pair_send, pair_recv, relay_send, relay_recv,
    direct_send, direct_recv, sum_send, sum_recv, weight_send, weight_recv,
):
    me = lax.axis_index("pos")
    ch = lax.axis_index("ch")
    core = lax.rem(ch, 2)
    row = ch // 2
    sibling = ch + 1 - 2 * core
    up = lax.rem(ch + 2, 2 * ring)
    down = lax.rem(ch + 2 * ring - 2, 2 * ring)
    row_up, row_down = lax.rem(row + 1, ring), lax.rem(row + ring - 1, ring)
    row_far = lax.rem(row + 2, ring)
    wide = even_ref.shape[1]
    piece = wide // PARTS
    rows_in = weight_ref.shape[0]
    pos_up, pos_down = lax.rem(me + 1, peers), lax.rem(me + peers - 1, peers)

    load_full = pltpu.make_async_copy(full_hbm, full, full_sem)
    load_full.start()

    barrier = pltpu.get_barrier_semaphore()

    def greet(off, carry):
        pl.semaphore_signal(barrier, inc=1, device_id={"pos": lax.rem(me + off, peers)}, device_id_type=MESH)
        return carry

    lax.fori_loop(1, peers, greet, 0)
    for other in (sibling, up, down):
        pl.semaphore_signal(barrier, inc=1, device_id={"ch": other}, device_id_type=MESH)
    pl.semaphore_wait(barrier, peers + 2)

    edge = halo_even.shape[1]
    to_up = pltpu.make_async_remote_copy(
        odd_ref.at[:, pl.ds(wide - edge, edge)], halo_odd, halo_send.at[0], halo_recv.at[0],
        device_id={"pos": pos_up}, device_id_type=MESH)
    to_down = pltpu.make_async_remote_copy(
        even_ref.at[:, pl.ds(0, edge)], halo_even, halo_send.at[1], halo_recv.at[1],
        device_id={"pos": pos_down}, device_id_type=MESH)
    to_up.start()
    to_down.start()
    taps[pl.ds(chan, chan), :] = even_ref[...]
    taps[pl.ds(2 * chan, chan), :] = odd_ref[...]
    spot = lax.broadcasted_iota(jnp.int32, (chan, wide), 1)
    moved_odd = pltpu.roll(odd_ref[...].astype(F32), 1, 1)
    moved_even = pltpu.roll(even_ref[...].astype(F32), wide - 1, 1)
    to_up.wait()
    to_down.wait()
    first = halo_odd[...].astype(F32)[:, edge - 1:edge] * jnp.where(me == 0, 0.0, 1.0)
    last = halo_even[...].astype(F32)[:, 0:1] * jnp.where(me == peers - 1, 0.0, 1.0)
    taps[pl.ds(0, chan), :] = jnp.where(spot == 0, first, moved_odd).astype(BF)
    taps[pl.ds(3 * chan, chan), :] = jnp.where(spot == wide - 1, last, moved_even).astype(BF)

    half = ring * chan

    def pair_copy(q):
        return pltpu.make_async_remote_copy(
            pair_out.at[q], pair_in.at[q], pair_send.at[q], pair_recv.at[q],
            device_id={"ch": sibling}, device_id_type=MESH)

    def relay_copy(q):
        return pltpu.make_async_remote_copy(
            part.at[q, row_far], relay.at[q], relay_send.at[q], relay_recv.at[q],
            device_id={"ch": up if q < PARTS // 2 else down}, device_id_type=MESH)

    def direct_copy(q):
        rising = q >= PARTS // 2
        return pltpu.make_async_remote_copy(
            part.at[q, row_up if rising else row_down], (before if rising else after).at[q],
            direct_send.at[q], direct_recv.at[q],
            device_id={"ch": up if rising else down}, device_id_type=MESH)

    def sum_copy(q):
        rising = q < PARTS // 2
        return pltpu.make_async_remote_copy(
            part.at[q, row_up if rising else row_down], (before if rising else after).at[q],
            sum_send.at[q], sum_recv.at[q],
            device_id={"ch": up if rising else down}, device_id_type=MESH)

    order = (0, PARTS // 2, 1, PARTS // 2 + 1)
    for q in order:
        block = taps[:, q * piece:(q + 1) * piece]
        pair_out[q] = jnp.dot(
            wt_ref[pl.ds((1 - core) * half, half), :], block, preferred_element_type=F32
        ).astype(BF).reshape(ring, chan, piece)
        pair_copy(q).start()
    for q in order:
        block = taps[:, q * piece:(q + 1) * piece]
        mine = jnp.dot(wt_ref[pl.ds(core * half, half), :], block, preferred_element_type=F32)
        pair_copy(q).wait_recv()
        both = mine.reshape(ring, chan, piece) + pair_in[q].astype(F32)
        exact[q] = both
        part[q] = both.astype(BF)
        relay_copy(q).start()
    for q in order:
        direct_copy(q).start()

    load_full.wait()
    for q in range(PARTS):
        where = slice(q * piece, (q + 1) * piece)
        term = lax.dot_general(full[:, where], taps[:, where], NT, preferred_element_type=F32)
        if q == 0:
            weight_acc[...] = term
        else:
            weight_acc[...] += term
    kept = weight_out.shape[1]
    for p in range(peers):
        weight_out[p] = jnp.concatenate(
            [weight_acc[p * rows_in:(p + 1) * rows_in, :],
             jnp.zeros((kept - rows_in, weight_acc.shape[1]), F32)], axis=0).astype(BF)

    def weight_copy(off):
        other = lax.rem(me + off, peers)
        return pltpu.make_async_remote_copy(
            weight_out.at[other], weight_in.at[me], weight_send.at[other], weight_recv.at[me],
            device_id={"pos": other}, device_id_type=MESH)

    def weight_start(off, carry):
        weight_copy(off).start()
        return carry

    lax.fori_loop(1, peers, weight_start, 0)

    for q in order:
        rising = q < PARTS // 2
        relay_copy(q).wait_recv()
        goal = row_up if rising else row_down
        part[q, goal] = (exact[q, goal] + relay[q].astype(F32)).astype(BF)
        sum_copy(q).start()
    for q in order:
        direct_copy(q).wait_recv()
        sum_copy(q).wait_recv()
        coarse_ref[:, q * piece:(q + 1) * piece] = (
            exact[q, row] + before[q].astype(F32) + after[q].astype(F32)).astype(BF)

    own = weight_out[me]
    weight_acc[pl.ds(0, kept), :] = own.astype(F32)

    def weight_add(off, carry):
        source = lax.rem(me + peers - off, peers)
        pltpu.make_async_remote_copy(
            weight_out.at[source], weight_in.at[source], weight_send.at[source], weight_recv.at[source],
            device_id={"pos": source}, device_id_type=MESH).wait_recv()
        weight_acc[pl.ds(0, kept), :] += weight_in[source].astype(F32)
        return carry

    lax.fori_loop(1, peers, weight_add, 0)
    weight_ref[...] = weight_acc[0:rows_in, :] * (1.0 / math.sqrt(total))

    for q in order:
        pair_copy(q).wait_send()
        relay_copy(q).wait_send()
        direct_copy(q).wait_send()
        sum_copy(q).wait_send()

    def weight_sent(off, carry):
        weight_copy(off).wait_send()
        return carry

    lax.fori_loop(1, peers, weight_sent, 0)


def tail(even, odd, wt, full, peers, ring, chan, total):
    wide = even.shape[1]
    piece = wide // PARTS
    channels = full.shape[0]
    rows_in = channels // peers
    kept = -(-rows_in // 16) * 16
    outs = KERNEL * chan
    edge = min(128, wide)
    dma = pltpu.SemaphoreType.DMA
    vmem = pl.BlockSpec(memory_space=pltpu.VMEM)
    return pl.pallas_call(
        functools.partial(tail_kernel, peers, ring, chan, total),
        out_shape=(jax.ShapeDtypeStruct((chan, wide), BF), jax.ShapeDtypeStruct((rows_in, outs), F32)),
        in_specs=[vmem, vmem, vmem, pl.BlockSpec(memory_space=pl.ANY)],
        out_specs=(vmem, vmem),
        scratch_shapes=[
            pltpu.VMEM((channels, wide), BF),
            pltpu.VMEM((outs, wide), BF),
            pltpu.VMEM((chan, edge), BF),
            pltpu.VMEM((chan, edge), BF),
            pltpu.VMEM((PARTS, ring, chan, piece), BF),
            pltpu.VMEM((PARTS, ring, chan, piece), BF),
            pltpu.VMEM((PARTS, ring, chan, piece), BF),
            pltpu.VMEM((PARTS, ring, chan, piece), F32),
            pltpu.VMEM((PARTS, chan, piece), BF),
            pltpu.VMEM((PARTS, chan, piece), BF),
            pltpu.VMEM((PARTS, chan, piece), BF),
            pltpu.VMEM((channels, outs), F32),
            pltpu.VMEM((peers, kept, outs), BF),
            pltpu.VMEM((peers, kept, outs), BF),
            dma, dma((2,)), dma((2,)), dma((PARTS,)), dma((PARTS,)), dma((PARTS,)), dma((PARTS,)),
            dma((PARTS,)), dma((PARTS,)), dma((PARTS,)), dma((PARTS,)), dma((peers,)), dma((peers,)),
        ],
        compiler_params=pltpu.CompilerParams(
            collective_id=1, has_side_effects=True, vmem_limit_bytes=56 * 1024 * 1024),
        cost_estimate=pl.CostEstimate(flops=4 * channels * outs * wide, bytes_accessed=2 * channels * wide * 2, transcendentals=0),
        name="tail",
    )(even, odd, wt, full)


def split_weight(tap_weight, ring, chan):
    taps, chan_local, channels = tap_weight.shape
    table = tap_weight.reshape(taps * chan_local, ring, 2, chan)
    return table.transpose(2, 1, 3, 0).reshape(channels, taps * chan_local)


FOLD = 8


def select_fold(prod, high, chan):
    kept = jnp.where(high == 0, prod[0:chan], 0.0)
    for g in range(1, FOLD):
        kept = kept + jnp.where(high == g, prod[g * chan:(g + 1) * chan], 0.0)
    return kept


def hot(mask):
    return jnp.where(mask, 1.0, 0.0).astype(BF)


def junction_kernel(
    peers, chan,
    act_hbm, track_hbm, owner_ref, acceptor_ref, donor_ref, score_ref,
    skip_ref, even_ref, odd_ref,
    act, track, acc, within_hot, terms, stack, wide_out, back,
    rows_out, rows_in, terms_out, terms_in, fetch_out, fetch_in,
    load_sem, rows_send, rows_recv, terms_send, terms_recv, fetch_send, fetch_recv,
):
    me = lax.axis_index("pos")
    count = owner_ref.shape[1]
    cap = within_hot.shape[0]
    fold = act.shape[1]
    per = fold.bit_length() - 1

    def load(which, hbm, ref, g):
        return pltpu.make_async_copy(
            hbm.at[:, pl.ds(g * fold, fold)], ref.at[pl.ds(g * chan, chan), :], load_sem.at[which, g])

    for g in range(FOLD):
        load(0, act_hbm, act, g).start()
    for g in range(FOLD):
        load(1, track_hbm, track, g).start()

    barrier = pltpu.get_barrier_semaphore()

    def greet(off, carry):
        pl.semaphore_signal(barrier, inc=1, device_id={"pos": lax.rem(me + off, peers)}, device_id_type=MESH)
        return carry

    lax.fori_loop(1, peers, greet, 0)

    owner = owner_ref[...]
    named = jnp.where(owner == lax.broadcasted_iota(jnp.int32, (peers, count), 0), 1.0, 0.0)
    earlier = hot(lax.broadcasted_iota(jnp.int32, (cap, cap), 0) < lax.broadcasted_iota(jnp.int32, (cap, cap), 1))
    carried = jnp.zeros((peers, 1), F32)
    for b in range(count // cap):
        part = named[:, b * cap:(b + 1) * cap]
        before = jnp.dot(part.astype(BF), earlier, preferred_element_type=F32) + carried
        within = jnp.sum(part * before, axis=0, keepdims=True).astype(jnp.int32)
        within_hot[:, b * cap:(b + 1) * cap] = hot(lax.broadcasted_iota(jnp.int32, (cap, cap), 0) == within)
        carried = carried + jnp.sum(part, axis=1, keepdims=True)
    wanted = acceptor_ref[...]
    planes = jnp.concatenate(
        [named * (wanted >> 7).astype(F32), named * (wanted & 127).astype(F32)], axis=0).astype(BF)
    slots = lax.dot_general(planes, within_hot[...], NT, preferred_element_type=F32)
    rows = (slots[0:peers] * 128.0 + slots[peers:2 * peers]).astype(jnp.int32)
    for p in range(peers):
        rows_out[p] = rows[p:p + 1, :]
    rows_in[me] = rows_out[me]

    pl.semaphore_wait(barrier, peers - 1)

    def send(kind, other):
        out, into, sent, got = (
            (rows_out, rows_in, rows_send, rows_recv),
            (terms_out, terms_in, terms_send, terms_recv),
            (fetch_out, fetch_in, fetch_send, fetch_recv),
        )[kind]
        return pltpu.make_async_remote_copy(
            out.at[other], into.at[me], sent.at[other], got.at[me],
            device_id={"pos": other}, device_id_type=MESH)

    def arrival(kind, other):
        out, into, sent, got = (
            (rows_out, rows_in, rows_send, rows_recv),
            (terms_out, terms_in, terms_send, terms_recv),
            (fetch_out, fetch_in, fetch_send, fetch_recv),
        )[kind]
        return pltpu.make_async_remote_copy(
            out.at[other], into.at[other], sent.at[other], got.at[other],
            device_id={"pos": other}, device_id_type=MESH)

    def each(first, body):
        def run(off, carry):
            body(off)
            return carry
        lax.fori_loop(first, peers, run, 0)

    each(1, lambda off: send(0, lax.rem(me + off, peers)).start())

    def gather(where):
        spot = lax.broadcasted_iota(jnp.int32, (fold, where.shape[1]), 0)
        prod = jnp.dot(act[...], hot(spot == (where & (fold - 1))), preferred_element_type=F32)
        return select_fold(prod, where >> per, chan)

    for g in range(FOLD):
        load(0, act_hbm, act, g).wait()

    def make_terms(b, carry):
        at = pl.ds(pl.multiple_of(b * cap, cap), cap)
        factor = score_ref[:, at] * (1.0 / math.sqrt(C))
        terms[:, at] = (gather(donor_ref[:, at]) * factor).astype(BF)
        return carry

    lax.fori_loop(0, count // cap, make_terms, 0)

    GROUP = 8

    def expand(group, carry):
        for k in range(GROUP):
            other = lax.rem(me + group * GROUP + k, peers)
            stack[k * chan:(k + 1) * chan, :] = terms[...] * hot(owner_ref[...] == other)
        slotted = lax.dot_general(stack[...], within_hot[...], NT, preferred_element_type=F32)
        for k in range(GROUP):
            other = lax.rem(me + group * GROUP + k, peers)
            terms_out[other] = slotted[k * chan:(k + 1) * chan, :].astype(BF)
        for k in range(GROUP):
            other = lax.rem(me + group * GROUP + k, peers)

            @pl.when(other != me)
            def _():
                send(1, other).start()
        return carry

    lax.fori_loop(0, peers // GROUP, expand, 0)
    terms_in[me] = terms_out[me]

    fetch_in[me] = gather(rows_in[me]).astype(BF)

    def answer(off):
        other = lax.rem(me + off, peers)
        arrival(0, other).wait_recv()
        fetch_out[other] = gather(rows_in[other]).astype(BF)
        send(2, other).start()

    each(1, answer)

    acc[...] = jnp.zeros_like(acc)
    step = min(256, fold)

    def scatter(values, where):
        n = where.shape[1]
        high, low = where >> per, where & (fold - 1)
        for g in range(FOLD):
            wide_out[g * chan:(g + 1) * chan, :] = values * hot(high == g)
        spot = lax.broadcasted_iota(jnp.int32, (step, n), 0)
        for r in range(fold // step):
            here = hot(spot + r * step == low)
            acc[:, r * step:(r + 1) * step] += lax.dot_general(
                wide_out[...], here, NT, preferred_element_type=F32)

    batch = wide_out.shape[1] // cap

    def add_terms(group, carry):
        values, where = [], []
        for k in range(batch):
            other = lax.rem(me + peers - (group * batch + k), peers)

            @pl.when(other != me)
            def _():
                arrival(1, other).wait_recv()
            values.append(terms_in[other])
            where.append(rows_in[other])
        scatter(jnp.concatenate(values, axis=1), jnp.concatenate(where, axis=1))
        return carry

    lax.fori_loop(0, peers // batch, add_terms, 0)

    back[...] = jnp.zeros_like(back)

    def collect(group, carry):
        blocks, names = [], []
        for k in range(GROUP):
            other = lax.rem(me + peers - (group * GROUP + k), peers)

            @pl.when(other != me)
            def _():
                arrival(2, other).wait_recv()
            blocks.append(fetch_in[other])
            names.append(other)
        block = jnp.concatenate(blocks, axis=0)
        for b in range(count // cap):
            at = slice(b * cap, (b + 1) * cap)
            prod = jnp.dot(block, within_hot[:, at], preferred_element_type=F32)
            owners = owner_ref[:, at]
            kept = back[:, at]
            for k in range(GROUP):
                kept = kept + jnp.where(owners == names[k], prod[k * chan:(k + 1) * chan], 0.0)
            back[:, at] = kept
        return carry

    lax.fori_loop(0, peers // GROUP, collect, 0)
    width = batch * cap
    for b in range(count // width):
        at = slice(b * width, (b + 1) * width)
        factor = score_ref[:, at] * (1.0 / math.sqrt(C))
        scatter((back[:, at] * factor).astype(BF), donor_ref[:, at])

    for g in range(FOLD):
        load(1, track_hbm, track, g).wait()
    pair = min(256, fold)
    spot = lax.broadcasted_iota(jnp.int32, (pair, pair), 0)
    goal = lax.broadcasted_iota(jnp.int32, (pair, pair), 1)
    half = pair // 2
    pick = hot(spot == jnp.where(goal < half, 2 * goal, 2 * (goal - half) + 1))
    for q in range(fold // pair):
        at = slice(q * pair, (q + 1) * pair)
        skip = (track[:, at].astype(F32) + acc[:, at]).astype(BF)
        split = jnp.dot(skip, pick, preferred_element_type=F32).astype(BF)
        for g in range(FOLD):
            rows_of = slice(g * chan, (g + 1) * chan)
            skip_ref[:, g * fold + q * pair:g * fold + (q + 1) * pair] = skip[rows_of]
            start = (g * fold + q * pair) // 2
            even_ref[:, start:start + half] = split[rows_of, :half]
            odd_ref[:, start:start + half] = split[rows_of, half:]

    def drain(off):
        other = lax.rem(me + off, peers)
        for kind in range(3):
            send(kind, other).wait_send()

    each(1, drain)


def junctions(activation, track_grad, owner, acceptor_row, donor_row, score_grad, peers):
    chan, length = activation.shape
    count = owner.shape[1]
    cap = count // 8
    fold = length // FOLD
    dma = pltpu.SemaphoreType.DMA
    vmem = pl.BlockSpec(memory_space=pltpu.VMEM)
    hbm = pl.BlockSpec(memory_space=pl.ANY)
    return pl.pallas_call(
        functools.partial(junction_kernel, peers, chan),
        out_shape=(
            jax.ShapeDtypeStruct((chan, length), BF),
            jax.ShapeDtypeStruct((chan, length // 2), BF),
            jax.ShapeDtypeStruct((chan, length // 2), BF),
        ),
        in_specs=[hbm, hbm, vmem, vmem, vmem, vmem],
        out_specs=(vmem, vmem, vmem),
        scratch_shapes=[
            pltpu.VMEM((FOLD * chan, fold), BF),
            pltpu.VMEM((FOLD * chan, fold), BF),
            pltpu.VMEM((FOLD * chan, fold), F32),
            pltpu.VMEM((cap, count), BF),
            pltpu.VMEM((chan, count), BF),
            pltpu.VMEM((8 * chan, count), BF),
            pltpu.VMEM((FOLD * chan, 4 * cap), BF),
            pltpu.VMEM((chan, count), F32),
            pltpu.VMEM((peers, 1, cap), jnp.int32),
            pltpu.VMEM((peers, 1, cap), jnp.int32),
            pltpu.VMEM((peers, chan, cap), BF),
            pltpu.VMEM((peers, chan, cap), BF),
            pltpu.VMEM((peers, chan, cap), BF),
            pltpu.VMEM((peers, chan, cap), BF),
            dma((2, FOLD)),
            dma((peers,)), dma((peers,)), dma((peers,)), dma((peers,)), dma((peers,)), dma((peers,)),
        ],
        compiler_params=pltpu.CompilerParams(
            collective_id=2, has_side_effects=True, vmem_limit_bytes=56 * 1024 * 1024),
        cost_estimate=pl.CostEstimate(flops=96 * 8 * 1024 * 256 * 768, bytes_accessed=8 * chan * length, transcendentals=0),
        name="junctions",
    )(activation, track_grad, owner, acceptor_row, donor_row, score_grad)


def shards(
    track_grad,
    activation,
    coarse_in,
    tap_weight,
    score_grad,
    donor_row,
    acceptor_owner,
    acceptor_row,
):
    peers, ring = lax.axis_size("pos"), lax.axis_size("ch") // 2
    chan_local = track_grad.shape[0]
    full_in = lax.all_gather(coarse_in, "ch", axis=0, tiled=True)
    wt = split_weight(tap_weight, ring, chan_local)
    skip_grad, even, odd = junctions(
        activation,
        track_grad,
        acceptor_owner.reshape(1, -1),
        acceptor_row.reshape(1, -1),
        donor_row.reshape(1, -1),
        score_grad.reshape(1, -1),
        peers,
    )
    coarse_grad, weight_rows = tail(
        even, odd, wt, full_in, peers, ring, chan_local, coarse_in.shape[1] * peers
    )
    weight_grad = weight_rows.reshape(-1, KERNEL, chan_local).transpose(1, 2, 0).astype(BF)
    return (skip_grad, coarse_grad, weight_grad)

def solution(mesh):
    in_specs = (
        P("ch", "pos"),
        P("ch", "pos"),
        P("ch", "pos"),
        P(None, "ch", None),
        P("pos"),
        P("pos"),
        P("pos", None),
        P("pos"),
    )
    out_specs = (P("ch", "pos"), P("ch", "pos"), P(None, "ch", "pos"))
    return jax.shard_map(shards, mesh=mesh, in_specs=in_specs, out_specs=out_specs, check_vma=False)
```

```python
import functools
import math

import jax
import jax.numpy as jnp
from jax import lax
from jax.experimental import pallas as pl
from jax.experimental.pallas import tpu as pltpu
from jax.sharding import PartitionSpec as P

C = 768
KERNEL = 4
FOLD = 8
PARTS = 4
GROUP = 8
BATCH = 4
BF = jnp.bfloat16
F32 = jnp.float32
MESH = pl.DeviceIdType.MESH
NT = (((1,), (1,)), ((), ()))


def hot(mask):
    return jnp.where(mask, 1.0, 0.0).astype(BF)


def iota(shape, dim):
    return lax.broadcasted_iota(jnp.int32, shape, dim)


def section_kernel(
    peers, inner, ring, total,
    act_hbm, track_hbm, coarse_hbm, weight_in_ref, owner_ref, acceptor_ref, donor_ref, score_ref,
    skip_ref, coarse_ref, weight_ref,
    act, track, acc, within_hot, terms, stack, spread, back,
    rows_out, rows_in, terms_out, terms_in, fetch_out, fetch_in,
    full, wt, taps, halo_even, halo_odd, pair_out, pair_in, part, exact, relay, before, after,
    weight_acc, first_out, first_in, second_out, second_in,
    load_sem, rows_send, rows_recv, terms_send, terms_recv, fetch_send, fetch_recv,
    gather_send, gather_recv, halo_send, halo_recv, pair_send, pair_recv, relay_send, relay_recv,
    direct_send, direct_recv, sum_send, sum_recv, first_send, first_recv, second_send, second_recv,
):
    me = lax.axis_index("pos")
    ch = lax.axis_index("ch")
    outer = peers // inner
    mine_out, mine_in = me // inner, lax.rem(me, inner)
    core, row = lax.rem(ch, 2), ch // 2
    sibling = ch + 1 - 2 * core
    up = lax.rem(ch + 2, 2 * ring)
    down = lax.rem(ch + 2 * ring - 2, 2 * ring)
    far = lax.rem(ch + 4, 2 * ring)
    row_up, row_down = lax.rem(row + 1, ring), lax.rem(row + ring - 1, ring)
    row_far = lax.rem(row + 2, ring)
    chan, wide = coarse_ref.shape
    piece = wide // PARTS
    count = owner_ref.shape[1]
    cap = within_hot.shape[0]
    fold = act.shape[1]
    per = fold.bit_length() - 1
    channels = full.shape[0]
    rows_each = channels // peers

    def load(which, hbm, ref, g):
        return pltpu.make_async_copy(
            hbm.at[:, pl.ds(g * fold, fold)], ref.at[pl.ds(g * chan, chan), :], load_sem.at[which, g])

    for g in range(FOLD):
        load(0, act_hbm, act, g).start()
    for g in range(FOLD):
        load(1, track_hbm, track, g).start()
    own_rows = pl.ds(pl.multiple_of(ch * chan, chan), chan)
    load_coarse = pltpu.make_async_copy(coarse_hbm, full.at[own_rows, :], load_sem.at[2, 0])
    load_coarse.start()

    def each(first, body):
        def run(off, carry):
            body(off)
            return carry
        lax.fori_loop(first, peers, run, 0)

    barrier = pltpu.get_barrier_semaphore()
    each(1, lambda off: pl.semaphore_signal(
        barrier, inc=1, device_id={"pos": lax.rem(me + off, peers)}, device_id_type=MESH))
    for other in (sibling, up, down, far):
        pl.semaphore_signal(barrier, inc=1, device_id={"ch": other}, device_id_type=MESH)

    owner = owner_ref[...]
    named = jnp.where(owner == iota((peers, count), 0), 1.0, 0.0)
    blocks = count // cap
    stacked = jnp.concatenate([named[:, b * cap:(b + 1) * cap] for b in range(blocks)], axis=0)
    ranks = jnp.dot(stacked.astype(BF), hot(iota((cap, cap), 0) < iota((cap, cap), 1)), preferred_element_type=F32)
    sums = jnp.sum(stacked, axis=1, keepdims=True)
    carried = jnp.zeros((peers, 1), F32)
    for b in range(blocks):
        at = slice(b * peers, (b + 1) * peers)
        within = jnp.sum(stacked[at] * (ranks[at] + carried), axis=0, keepdims=True).astype(jnp.int32)
        within_hot[:, b * cap:(b + 1) * cap] = hot(iota((cap, cap), 0) == within)
        carried = carried + sums[at]
    wanted = acceptor_ref[...]
    planes = jnp.concatenate(
        [named * (wanted >> 7).astype(F32), named * (wanted & 127).astype(F32)], axis=0).astype(BF)
    slots = lax.dot_general(planes, within_hot[...], NT, preferred_element_type=F32)
    rows = (slots[0:peers] * 128.0 + slots[peers:2 * peers]).astype(jnp.int32)
    for p in range(peers):
        rows_out[p] = rows[p:p + 1, :]
    rows_in[me] = rows_out[me]

    pl.semaphore_wait(barrier, peers + 3)

    kinds = (
        (rows_out, rows_in, rows_send, rows_recv),
        (terms_out, terms_in, terms_send, terms_recv),
        (fetch_out, fetch_in, fetch_send, fetch_recv),
    )

    def send(kind, other):
        out, into, sent, got = kinds[kind]
        return pltpu.make_async_remote_copy(
            out.at[other], into.at[me], sent.at[other], got.at[me],
            device_id={"pos": other}, device_id_type=MESH)

    def arrival(kind, other):
        out, into, sent, got = kinds[kind]
        return pltpu.make_async_remote_copy(
            out.at[other], into.at[other], sent.at[other], got.at[other],
            device_id={"pos": other}, device_id_type=MESH)

    each(1, lambda off: send(0, lax.rem(me + off, peers)).start())

    def share(n, source, goal):
        span = pl.ds(pl.multiple_of(source * chan, chan), chan)
        return pltpu.make_async_remote_copy(
            coarse_hbm if n < 4 else full.at[span, :], full.at[span, :], gather_send.at[n], gather_recv.at[source],
            device_id={"ch": goal}, device_id_type=MESH)

    for n, goal in enumerate((up, down, far, sibling)):
        share(n, ch, goal).start()

    def shared(source):
        span = pl.ds(pl.multiple_of(source * chan, chan), chan)
        return pltpu.make_async_remote_copy(
            full.at[span, :], full.at[span, :], gather_send.at[0], gather_recv.at[source],
            device_id={"ch": sibling}, device_id_type=MESH)

    def gather(where):
        spot = iota((fold, where.shape[1]), 0)
        prod = jnp.dot(act[...], hot(spot == (where & (fold - 1))), preferred_element_type=F32)
        high = where >> per
        kept = jnp.where(high == 0, prod[0:chan], 0.0)
        for g in range(1, FOLD):
            kept = kept + jnp.where(high == g, prod[g * chan:(g + 1) * chan], 0.0)
        return kept

    for g in range(FOLD):
        load(0, act_hbm, act, g).wait()

    def make_terms(b, carry):
        at = pl.ds(pl.multiple_of(b * cap, cap), cap)
        factor = score_ref[:, at] * (1.0 / math.sqrt(C))
        terms[:, at] = (gather(donor_ref[:, at]) * factor).astype(BF)
        return carry

    lax.fori_loop(0, blocks, make_terms, 0)

    def answer(off):
        other = lax.rem(me + off, peers)
        arrival(0, other).wait_recv()
        fetch_out[other] = gather(rows_in[other]).astype(BF)
        send(2, other).start()

    each(1, answer)
    fetch_in[me] = gather(rows_in[me]).astype(BF)

    def expand(group, carry):
        for k in range(GROUP):
            other = lax.rem(me + group * GROUP + k, peers)
            stack[k * chan:(k + 1) * chan, :] = terms[...] * hot(owner_ref[...] == other)
        slotted = lax.dot_general(stack[...], within_hot[...], NT, preferred_element_type=F32)
        for k in range(GROUP):
            other = lax.rem(me + group * GROUP + k, peers)
            terms_out[other] = slotted[k * chan:(k + 1) * chan, :].astype(BF)

            @pl.when(other != me)
            def _():
                send(1, other).start()
        return carry

    lax.fori_loop(0, peers // GROUP, expand, 0)
    terms_in[me] = terms_out[me]

    for g in range(FOLD):
        load(1, track_hbm, track, g).wait()
    acc[...] = track[...].astype(F32)
    for k in range(KERNEL):
        turned = weight_in_ref[k].astype(F32).T.astype(BF)
        for r in range(ring):
            for c in range(2):
                wt[(c * ring + r) * chan:(c * ring + r + 1) * chan, k * chan:(k + 1) * chan] = (
                    turned[(2 * r + c) * chan:(2 * r + c + 1) * chan])
    back[...] = jnp.zeros_like(back)

    def collect(group, carry):
        held, names = [], []
        for k in range(GROUP):
            other = lax.rem(me + peers - (group * GROUP + k), peers)

            @pl.when(other != me)
            def _():
                arrival(2, other).wait_recv()
            held.append(fetch_in[other])
            names.append(other)
        block = jnp.concatenate(held, axis=0)
        for b in range(blocks):
            at = slice(b * cap, (b + 1) * cap)
            prod = jnp.dot(block, within_hot[:, at], preferred_element_type=F32)
            owners = owner_ref[:, at]
            kept = back[:, at]
            for k in range(GROUP):
                kept = kept + jnp.where(owners == names[k], prod[k * chan:(k + 1) * chan], 0.0)
            back[:, at] = kept
        return carry

    lax.fori_loop(0, peers // GROUP, collect, 0)

    for n, source in enumerate((up, down, far)):
        shared(source).wait_recv()
        share(4 + n, source, sibling).start()

    step = min(256, fold)

    def scatter(values, where):
        n = where.shape[1]
        high, low = where >> per, where & (fold - 1)
        for g in range(FOLD):
            spread[g * chan:(g + 1) * chan, :] = values * hot(high == g)
        for r in range(fold // step):
            here = hot(iota((step, n), 0) + r * step == low)
            acc[:, r * step:(r + 1) * step] += lax.dot_general(
                spread[...], here, NT, preferred_element_type=F32)

    width = BATCH * cap

    def add_back(b, carry):
        at = pl.ds(pl.multiple_of(b * width, width), width)
        factor = score_ref[:, at] * (1.0 / math.sqrt(C))
        scatter((back[:, at] * factor).astype(BF), donor_ref[:, at])
        return carry

    lax.fori_loop(0, count // width, add_back, 0)

    def add_terms(group, carry):
        values, where = [], []
        for k in range(BATCH):
            other = lax.rem(me + peers - (group * BATCH + k), peers)

            @pl.when(other != me)
            def _():
                arrival(1, other).wait_recv()
            values.append(terms_in[other])
            where.append(rows_in[other])
        scatter(jnp.concatenate(values, axis=1), jnp.concatenate(where, axis=1))
        return carry

    lax.fori_loop(0, peers // BATCH, add_terms, 0)

    pair = min(256, fold)
    half_pair = pair // 2
    goal = iota((pair, pair), 1)
    pick = hot(iota((pair, pair), 0) == jnp.where(goal < half_pair, 2 * goal, 2 * (goal - half_pair) + 1))
    edge = halo_even.shape[1]
    to_up = pltpu.make_async_remote_copy(
        taps.at[pl.ds(2 * chan, chan), pl.ds(wide - edge, edge)], halo_odd, halo_send.at[0], halo_recv.at[0],
        device_id={"pos": lax.rem(me + 1, peers)}, device_id_type=MESH)
    to_down = pltpu.make_async_remote_copy(
        taps.at[pl.ds(chan, chan), pl.ds(0, edge)], halo_even, halo_send.at[1], halo_recv.at[1],
        device_id={"pos": lax.rem(me + peers - 1, peers)}, device_id_type=MESH)
    last_q = fold // pair - 1
    for q in [0, last_q] + list(range(1, last_q)):
        at = slice(q * pair, (q + 1) * pair)
        skip = acc[:, at].astype(BF)
        split = jnp.dot(skip, pick, preferred_element_type=F32).astype(BF)
        for g in range(FOLD):
            rows_of = slice(g * chan, (g + 1) * chan)
            skip_ref[:, g * fold + q * pair:g * fold + (q + 1) * pair] = skip[rows_of]
            start = (g * fold + q * pair) // 2
            taps[chan:2 * chan, start:start + half_pair] = split[rows_of, :half_pair]
            taps[2 * chan:3 * chan, start:start + half_pair] = split[rows_of, half_pair:]
        if q == last_q:
            to_down.start()
            to_up.start()
    spot = iota((chan, wide), 1)
    taps[0:chan, :] = pltpu.roll(taps[2 * chan:3 * chan, :].astype(F32), 1, 1).astype(BF)
    taps[3 * chan:4 * chan, :] = pltpu.roll(taps[chan:2 * chan, :].astype(F32), wide - 1, 1).astype(BF)

    half = ring * chan

    def pair_copy(q):
        return pltpu.make_async_remote_copy(
            pair_out.at[q], pair_in.at[q], pair_send.at[q], pair_recv.at[q],
            device_id={"ch": sibling}, device_id_type=MESH)

    def relay_copy(q):
        return pltpu.make_async_remote_copy(
            part.at[q, row_far], relay.at[q], relay_send.at[q], relay_recv.at[q],
            device_id={"ch": up if q < PARTS // 2 else down}, device_id_type=MESH)

    def direct_copy(q):
        rising = q >= PARTS // 2
        return pltpu.make_async_remote_copy(
            part.at[q, row_up if rising else row_down], (before if rising else after).at[q],
            direct_send.at[q], direct_recv.at[q],
            device_id={"ch": up if rising else down}, device_id_type=MESH)

    def sum_copy(q):
        rising = q < PARTS // 2
        return pltpu.make_async_remote_copy(
            part.at[q, row_up if rising else row_down], (before if rising else after).at[q],
            sum_send.at[q], sum_recv.at[q],
            device_id={"ch": up if rising else down}, device_id_type=MESH)

    def columns(q):
        return slice(q * piece, (q + 1) * piece)

    def for_sibling(q):
        pair_out[q] = jnp.dot(
            wt[pl.ds(pl.multiple_of((1 - core) * half, half), half), :], taps[:, columns(q)], preferred_element_type=F32
        ).astype(BF).reshape(ring, chan, piece)
        pair_copy(q).start()

    def for_ring(q):
        mine = jnp.dot(
            wt[pl.ds(pl.multiple_of(core * half, half), half), :], taps[:, columns(q)], preferred_element_type=F32)
        pair_copy(q).wait_recv()
        both = mine.reshape(ring, chan, piece) + pair_in[q].astype(F32)
        exact[q] = both
        part[q] = both.astype(BF)
        relay_copy(q).start()

    order = (1, 2, 0, 3)
    for_sibling(1)
    for_sibling(2)
    for_ring(1)
    to_up.wait()
    to_down.wait()
    first = halo_odd[...].astype(F32)[:, edge - 1:edge] * jnp.where(me == 0, 0.0, 1.0)
    last = halo_even[...].astype(F32)[:, 0:1] * jnp.where(me == peers - 1, 0.0, 1.0)
    lane = iota((chan, edge), 1)
    taps[0:chan, 0:edge] = jnp.where(lane == 0, first, taps[0:chan, 0:edge].astype(F32)).astype(BF)
    taps[3 * chan:4 * chan, wide - edge:wide] = jnp.where(
        lane == edge - 1, last, taps[3 * chan:4 * chan, wide - edge:wide].astype(F32)).astype(BF)
    for_sibling(0)
    for_ring(2)
    for_sibling(3)
    for_ring(0)
    for_ring(3)
    for q in order:
        direct_copy(q).start()

    load_coarse.wait()
    for source in (sibling, lax.rem(sibling + 2, 2 * ring), lax.rem(sibling + 4, 2 * ring), lax.rem(sibling + 6, 2 * ring)):
        shared(source).wait_recv()
    for q in range(PARTS):
        term = lax.dot_general(full[:, columns(q)], taps[:, columns(q)], NT, preferred_element_type=F32)
        if q == 0:
            weight_acc[...] = term
        else:
            weight_acc[...] += term
    group_rows = channels // outer
    for x in range(outer):
        first_out[x] = weight_acc[x * group_rows:(x + 1) * group_rows, :].astype(BF)

    def first_copy(off):
        other = lax.rem(mine_out + off, outer)
        return pltpu.make_async_remote_copy(
            first_out.at[other], first_in.at[mine_out], first_send.at[other], first_recv.at[mine_out],
            device_id={"pos": other * inner + mine_in}, device_id_type=MESH)

    def first_arrival(off):
        source = lax.rem(mine_out + off, outer)
        return pltpu.make_async_remote_copy(
            first_out.at[source], first_in.at[source], first_send.at[source], first_recv.at[source],
            device_id={"pos": source * inner + mine_in}, device_id_type=MESH), source

    def second_copy(off):
        other = lax.rem(mine_in + off, inner)
        return pltpu.make_async_remote_copy(
            second_out.at[other], second_in.at[mine_in], second_send.at[other], second_recv.at[mine_in],
            device_id={"pos": mine_out * inner + other}, device_id_type=MESH)

    def second_arrival(off):
        source = lax.rem(mine_in + off, inner)
        return pltpu.make_async_remote_copy(
            second_out.at[source], second_in.at[source], second_send.at[source], second_recv.at[source],
            device_id={"pos": mine_out * inner + source}, device_id_type=MESH), source

    for off in range(1, outer):
        first_copy(off).start()

    def pass_on(q):
        rising = q < PARTS // 2
        relay_copy(q).wait_recv()
        to = row_up if rising else row_down
        part[q, to] = (exact[q, to] + relay[q].astype(F32)).astype(BF)
        sum_copy(q).start()

    pass_on(order[0])
    pass_on(order[1])

    partial = weight_acc[pl.ds(pl.multiple_of(mine_out * group_rows, group_rows), group_rows), :]
    for off in range(1, outer):
        came, source = first_arrival(off)
        came.wait_recv()
        partial = partial + first_in[source].astype(F32)
    kept = second_out.shape[1]
    blank = jnp.zeros((kept - rows_each, partial.shape[1]), F32)
    for z in range(inner):
        second_out[z] = jnp.concatenate([partial[z * rows_each:(z + 1) * rows_each], blank], axis=0).astype(BF)
    for off in range(1, inner):
        second_copy(off).start()

    pass_on(order[2])
    pass_on(order[3])

    done = second_out[mine_in].astype(F32)
    for off in range(1, inner):
        came, source = second_arrival(off)
        came.wait_recv()
        done = done + second_in[source].astype(F32)
    done = done * (1.0 / math.sqrt(total))
    fill = jnp.zeros((128 - kept, done.shape[1]), F32)
    turned = jnp.concatenate([done, fill], axis=0).T[:, 0:rows_each]
    for k in range(KERNEL):
        weight_ref[k] = turned[k * chan:(k + 1) * chan].astype(BF)

    for q in order:
        direct_copy(q).wait_recv()
        sum_copy(q).wait_recv()
        coarse_ref[:, columns(q)] = (exact[q, row] + before[q].astype(F32) + after[q].astype(F32)).astype(BF)

    for n, to in enumerate((up, down, far, sibling)):
        share(n, ch, to).wait_send()
    for n, source in enumerate((up, down, far)):
        share(4 + n, source, sibling).wait_send()

    def drain(off):
        other = lax.rem(me + off, peers)
        for kind in range(3):
            send(kind, other).wait_send()

    each(1, drain)
    for q in order:
        pair_copy(q).wait_send()
        relay_copy(q).wait_send()
        direct_copy(q).wait_send()
        sum_copy(q).wait_send()
    for off in range(1, outer):
        first_copy(off).wait_send()
    for off in range(1, inner):
        second_copy(off).wait_send()


def section(track_grad, activation, coarse_in, tap_weight, score_grad, donor_row, owner, acceptor_row, peers, ring):
    chan, length = activation.shape
    wide = coarse_in.shape[1]
    channels = tap_weight.shape[2]
    count = owner.shape[1]
    cap = count // 8
    fold = length // FOLD
    piece = wide // PARTS
    inner = min(8, peers // 2)
    outer = peers // inner
    outs = KERNEL * chan
    rows_each = channels // peers
    kept = -(-rows_each // 16) * 16
    edge = min(128, wide)
    dma = pltpu.SemaphoreType.DMA
    vmem = pl.BlockSpec(memory_space=pltpu.VMEM)
    hbm = pl.BlockSpec(memory_space=pl.ANY)
    slots = pltpu.VMEM((peers, chan, cap), BF)
    names = pltpu.VMEM((peers, 1, cap), jnp.int32)
    quarter = pltpu.VMEM((PARTS, ring, chan, piece), BF)
    eighth = pltpu.VMEM((PARTS, chan, piece), BF)
    return pl.pallas_call(
        functools.partial(section_kernel, peers, inner, ring, wide * peers),
        out_shape=(
            jax.ShapeDtypeStruct((chan, length), BF),
            jax.ShapeDtypeStruct((chan, wide), BF),
            jax.ShapeDtypeStruct((KERNEL, chan, rows_each), BF),
        ),
        in_specs=[hbm, hbm, hbm, vmem, vmem, vmem, vmem, vmem],
        out_specs=(vmem, vmem, vmem),
        scratch_shapes=[
            pltpu.VMEM((FOLD * chan, fold), BF),
            pltpu.VMEM((FOLD * chan, fold), BF),
            pltpu.VMEM((FOLD * chan, fold), F32),
            pltpu.VMEM((cap, count), BF),
            pltpu.VMEM((chan, count), BF),
            pltpu.VMEM((GROUP * chan, count), BF),
            pltpu.VMEM((FOLD * chan, BATCH * cap), BF),
            pltpu.VMEM((chan, count), F32),
            names, names, slots, slots, slots, slots,
            pltpu.VMEM((channels, wide), BF),
            pltpu.VMEM((channels, outs), BF),
            pltpu.VMEM((outs, wide), BF),
            pltpu.VMEM((chan, edge), BF),
            pltpu.VMEM((chan, edge), BF),
            quarter, quarter, quarter,
            pltpu.VMEM((PARTS, ring, chan, piece), F32),
            eighth, eighth, eighth,
            pltpu.VMEM((channels, outs), F32),
            pltpu.VMEM((outer, channels // outer, outs), BF),
            pltpu.VMEM((outer, channels // outer, outs), BF),
            pltpu.VMEM((inner, kept, outs), BF),
            pltpu.VMEM((inner, kept, outs), BF),
            dma((3, FOLD)),
            dma((peers,)), dma((peers,)), dma((peers,)), dma((peers,)), dma((peers,)), dma((peers,)),
            dma((7,)), dma((2 * ring,)), dma((2,)), dma((2,)),
            dma((PARTS,)), dma((PARTS,)), dma((PARTS,)), dma((PARTS,)),
            dma((PARTS,)), dma((PARTS,)), dma((PARTS,)), dma((PARTS,)),
            dma((outer,)), dma((outer,)), dma((inner,)), dma((inner,)),
        ],
        compiler_params=pltpu.CompilerParams(
            collective_id=1, has_side_effects=True, vmem_limit_bytes=60 * 1024 * 1024),
        name="section",
    )(activation, track_grad, coarse_in, tap_weight, owner, acceptor_row, donor_row, score_grad)


def shards(
    track_grad,
    activation,
    coarse_in,
    tap_weight,
    score_grad,
    donor_row,
    acceptor_owner,
    acceptor_row,
):
    return section(
        track_grad,
        activation,
        coarse_in,
        tap_weight,
        score_grad.reshape(1, -1),
        donor_row.reshape(1, -1),
        acceptor_owner.reshape(1, -1),
        acceptor_row.reshape(1, -1),
        lax.axis_size("pos"),
        lax.axis_size("ch") // 2,
    )


def solution(mesh):
    in_specs = (
        P("ch", "pos"),
        P("ch", "pos"),
        P("ch", "pos"),
        P(None, "ch", None),
        P("pos"),
        P("pos"),
        P("pos", None),
        P("pos"),
    )
    out_specs = (P("ch", "pos"), P("ch", "pos"), P(None, "ch", "pos"))
    return jax.shard_map(shards, mesh=mesh, in_specs=in_specs, out_specs=out_specs, check_vma=False)
```

```python
import functools
import math

import jax
import jax.numpy as jnp
from jax import lax
from jax.experimental import pallas as pl
from jax.experimental.pallas import tpu as pltpu
from jax.sharding import PartitionSpec as P

C = 768
KERNEL = 4
FOLD = 8
PARTS = 8
GROUP = 8
BATCH = 4
BF = jnp.bfloat16
F32 = jnp.float32
MESH = pl.DeviceIdType.MESH
NT = (((1,), (1,)), ((), ()))


def hot(mask):
    return jnp.where(mask, 1.0, 0.0).astype(BF)


def iota(shape, dim):
    return lax.broadcasted_iota(jnp.int32, shape, dim)


def section_kernel(
    peers, inner, ring, total,
    act_hbm, track_hbm, coarse_hbm, weight_in_ref, owner_ref, acceptor_ref, donor_ref, score_ref,
    skip_hbm, out_hbm, weight_ref,
    skip_ref, coarse_ref, act, track, acc, within_hot, terms, stack, spread, back,
    rows_out, rows_in, terms_out, terms_in, fetch_out, fetch_in,
    full, wt, taps, halo_even, halo_odd, pair_out, pair_in, part, exact, relay, before, after,
    weight_acc, first_out, first_in, second_out, second_in,
    load_sem, rows_send, rows_recv, terms_send, terms_recv, fetch_send, fetch_recv,
    gather_send, gather_recv, halo_send, halo_recv, pair_send, pair_recv, relay_send, relay_recv,
    direct_send, direct_recv, sum_send, sum_recv, first_send, first_recv, second_send, second_recv, store_sem,
):
    me = lax.axis_index("pos")
    ch = lax.axis_index("ch")
    outer = peers // inner
    mine_out, mine_in = me // inner, lax.rem(me, inner)
    core, row = lax.rem(ch, 2), ch // 2
    sibling = ch + 1 - 2 * core
    up = lax.rem(ch + 2, 2 * ring)
    down = lax.rem(ch + 2 * ring - 2, 2 * ring)
    far = lax.rem(ch + 4, 2 * ring)
    row_up, row_down = lax.rem(row + 1, ring), lax.rem(row + ring - 1, ring)
    row_far = lax.rem(row + 2, ring)
    chan, wide = coarse_ref.shape
    piece = wide // PARTS
    count = owner_ref.shape[1]
    cap = within_hot.shape[0]
    fold = act.shape[1]
    per = fold.bit_length() - 1
    channels = full.shape[0]
    rows_each = channels // peers

    def load(which, hbm, ref, g):
        return pltpu.make_async_copy(
            hbm.at[:, pl.ds(g * fold, fold)], ref.at[pl.ds(g * chan, chan), :], load_sem.at[which, g])

    for g in range(FOLD):
        load(0, act_hbm, act, g).start()
    for g in range(FOLD):
        load(1, track_hbm, track, g).start()
    own_rows = pl.ds(pl.multiple_of(ch * chan, chan), chan)
    load_coarse = pltpu.make_async_copy(coarse_hbm, full.at[own_rows, :], load_sem.at[2, 0])
    load_coarse.start()

    def each(first, body):
        def run(off, carry):
            body(off)
            return carry
        lax.fori_loop(first, peers, run, 0)

    barrier = pltpu.get_barrier_semaphore()
    each(1, lambda off: pl.semaphore_signal(
        barrier, inc=1, device_id={"pos": lax.rem(me + off, peers)}, device_id_type=MESH))
    for other in (sibling, up, down, far):
        pl.semaphore_signal(barrier, inc=1, device_id={"ch": other}, device_id_type=MESH)

    owner = owner_ref[...]
    named = jnp.where(owner == iota((peers, count), 0), 1.0, 0.0)
    blocks = count // cap
    stacked = jnp.concatenate([named[:, b * cap:(b + 1) * cap] for b in range(blocks)], axis=0)
    ranks = jnp.dot(stacked.astype(BF), hot(iota((cap, cap), 0) < iota((cap, cap), 1)), preferred_element_type=F32)
    sums = jnp.sum(stacked, axis=1, keepdims=True)
    carried = jnp.zeros((peers, 1), F32)
    for b in range(blocks):
        at = slice(b * peers, (b + 1) * peers)
        within = jnp.sum(stacked[at] * (ranks[at] + carried), axis=0, keepdims=True).astype(jnp.int32)
        within_hot[:, b * cap:(b + 1) * cap] = hot(iota((cap, cap), 0) == within)
        carried = carried + sums[at]
    wanted = acceptor_ref[...]
    planes = jnp.concatenate(
        [named * (wanted >> 7).astype(F32), named * (wanted & 127).astype(F32)], axis=0).astype(BF)
    slots = lax.dot_general(planes, within_hot[...], NT, preferred_element_type=F32)
    rows = (slots[0:peers] * 128.0 + slots[peers:2 * peers]).astype(jnp.int32)
    for p in range(peers):
        rows_out[p] = rows[p:p + 1, :]
    rows_in[me] = rows_out[me]

    def gather(where):
        spot = iota((fold, where.shape[1]), 0)
        prod = jnp.dot(act[...], hot(spot == (where & (fold - 1))), preferred_element_type=F32)
        high = where >> per
        kept = jnp.where(high == 0, prod[0:chan], 0.0)
        for g in range(1, FOLD):
            kept = kept + jnp.where(high == g, prod[g * chan:(g + 1) * chan], 0.0)
        return kept

    for g in range(FOLD):
        load(0, act_hbm, act, g).wait()

    def make_terms(b, carry):
        at = pl.ds(pl.multiple_of(b * cap, cap), cap)
        factor = score_ref[:, at] * (1.0 / math.sqrt(C))
        terms[:, at] = (gather(donor_ref[:, at]) * factor).astype(BF)
        return carry

    lax.fori_loop(0, blocks, make_terms, 0)

    def expand(group):
        for k in range(GROUP):
            other = lax.rem(me + group * GROUP + k, peers)
            stack[k * chan:(k + 1) * chan, :] = terms[...] * hot(owner_ref[...] == other)
        slotted = lax.dot_general(stack[...], within_hot[...], NT, preferred_element_type=F32)
        for k in range(GROUP):
            other = lax.rem(me + group * GROUP + k, peers)
            terms_out[other] = slotted[k * chan:(k + 1) * chan, :].astype(BF)

    def leave(group, first):
        for k in range(first, GROUP):
            send(1, lax.rem(me + group * GROUP + k, peers)).start()

    def expand_next(group, carry):
        expand(group)
        leave(group, 0)
        return carry

    expand(0)
    terms_in[me] = terms_out[me]

    pl.semaphore_wait(barrier, peers + 3)

    kinds = (
        (rows_out, rows_in, rows_send, rows_recv),
        (terms_out, terms_in, terms_send, terms_recv),
        (fetch_out, fetch_in, fetch_send, fetch_recv),
    )

    def send(kind, other):
        out, into, sent, got = kinds[kind]
        return pltpu.make_async_remote_copy(
            out.at[other], into.at[me], sent.at[other], got.at[me],
            device_id={"pos": other}, device_id_type=MESH)

    def arrival(kind, other):
        out, into, sent, got = kinds[kind]
        return pltpu.make_async_remote_copy(
            out.at[other], into.at[other], sent.at[other], got.at[other],
            device_id={"pos": other}, device_id_type=MESH)

    each(1, lambda off: send(0, lax.rem(me + off, peers)).start())

    leave(0, 1)

    def share(n, source, goal):
        span = pl.ds(pl.multiple_of(source * chan, chan), chan)
        return pltpu.make_async_remote_copy(
            coarse_hbm if n < 4 else full.at[span, :], full.at[span, :], gather_send.at[n], gather_recv.at[source],
            device_id={"ch": goal}, device_id_type=MESH)

    for n, goal in enumerate((up, down, far, sibling)):
        share(n, ch, goal).start()

    def shared(source):
        span = pl.ds(pl.multiple_of(source * chan, chan), chan)
        return pltpu.make_async_remote_copy(
            full.at[span, :], full.at[span, :], gather_send.at[0], gather_recv.at[source],
            device_id={"ch": sibling}, device_id_type=MESH)

    def answer(off):
        other = lax.rem(me + off, peers)
        arrival(0, other).wait_recv()
        fetch_out[other] = gather(rows_in[other]).astype(BF)
        send(2, other).start()

    each(1, answer)
    fetch_in[me] = gather(rows_in[me]).astype(BF)

    lax.fori_loop(1, peers // GROUP, expand_next, 0)

    for g in range(FOLD):
        load(1, track_hbm, track, g).wait()
    acc[...] = track[...].astype(F32)
    for k in range(KERNEL):
        turned = weight_in_ref[k].astype(F32).T.astype(BF)
        for r in range(ring):
            for c in range(2):
                wt[(c * ring + r) * chan:(c * ring + r + 1) * chan, k * chan:(k + 1) * chan] = (
                    turned[(2 * r + c) * chan:(2 * r + c + 1) * chan])
    back[...] = jnp.zeros_like(back)

    def collect(group, carry):
        held, names = [], []
        for k in range(GROUP):
            other = lax.rem(me + peers - (group * GROUP + k), peers)

            @pl.when(other != me)
            def _():
                arrival(2, other).wait_recv()
            held.append(fetch_in[other])
            names.append(other)
        block = jnp.concatenate(held, axis=0)
        for b in range(blocks):
            at = slice(b * cap, (b + 1) * cap)
            prod = jnp.dot(block, within_hot[:, at], preferred_element_type=F32)
            owners = owner_ref[:, at]
            kept = back[:, at]
            for k in range(GROUP):
                kept = kept + jnp.where(owners == names[k], prod[k * chan:(k + 1) * chan], 0.0)
            back[:, at] = kept
        return carry

    lax.fori_loop(0, peers // GROUP, collect, 0)

    for n, source in enumerate((up, down, far)):
        shared(source).wait_recv()
        share(4 + n, source, sibling).start()

    step = min(256, fold)

    def scatter(values, where):
        n = where.shape[1]
        high, low = where >> per, where & (fold - 1)
        for g in range(FOLD):
            spread[g * chan:(g + 1) * chan, 0:n] = values * hot(high == g)
        for r in range(fold // step):
            here = hot(iota((step, n), 0) + r * step == low)
            acc[:, r * step:(r + 1) * step] += lax.dot_general(
                spread[:, 0:n], here, NT, preferred_element_type=F32)

    width = BATCH * cap

    def add_back(b, carry):
        at = pl.ds(pl.multiple_of(b * width, width), width)
        factor = score_ref[:, at] * (1.0 / math.sqrt(C))
        scatter((back[:, at] * factor).astype(BF), donor_ref[:, at])
        return carry

    lax.fori_loop(0, count // width, add_back, 0)

    def add_terms(start, size):
        values, where = [], []
        for k in range(size):
            other = lax.rem(me + 2 * peers - (start + k), peers)

            @pl.when(other != me)
            def _():
                arrival(1, other).wait_recv()
            values.append(terms_in[other])
            where.append(rows_in[other])
        scatter(jnp.concatenate(values, axis=1), jnp.concatenate(where, axis=1))

    def add_batch(group, carry):
        add_terms(group * BATCH, BATCH)
        return carry

    lax.fori_loop(0, peers // BATCH - 1, add_batch, 0)
    add_terms(peers - BATCH, BATCH // 2)
    add_terms(peers - BATCH // 2, BATCH // 2)

    pair = min(256, fold)
    half_pair = pair // 2
    goal = iota((pair, pair), 1)
    pick = hot(iota((pair, pair), 0) == jnp.where(goal < half_pair, 2 * goal, 2 * (goal - half_pair) + 1))
    edge = halo_even.shape[1]
    to_up = pltpu.make_async_remote_copy(
        taps.at[pl.ds(2 * chan, chan), pl.ds(wide - edge, edge)], halo_odd, halo_send.at[0], halo_recv.at[0],
        device_id={"pos": lax.rem(me + 1, peers)}, device_id_type=MESH)
    to_down = pltpu.make_async_remote_copy(
        taps.at[pl.ds(chan, chan), pl.ds(0, edge)], halo_even, halo_send.at[1], halo_recv.at[1],
        device_id={"pos": lax.rem(me + peers - 1, peers)}, device_id_type=MESH)
    last_q = fold // pair - 1
    for q in [0, last_q] + list(range(1, last_q)):
        at = slice(q * pair, (q + 1) * pair)
        skip = acc[:, at].astype(BF)
        split = jnp.dot(skip, pick, preferred_element_type=F32).astype(BF)
        for g in range(FOLD):
            rows_of = slice(g * chan, (g + 1) * chan)
            skip_ref[:, g * fold + q * pair:g * fold + (q + 1) * pair] = skip[rows_of]
            start = (g * fold + q * pair) // 2
            taps[chan:2 * chan, start:start + half_pair] = split[rows_of, :half_pair]
            taps[2 * chan:3 * chan, start:start + half_pair] = split[rows_of, half_pair:]
        if q == last_q:
            to_down.start()
            to_up.start()
    store_skip = pltpu.make_async_copy(skip_ref, skip_hbm, store_sem.at[0])
    store_skip.start()
    taps[0:chan, :] = pltpu.roll(taps[2 * chan:3 * chan, :].astype(F32), 1, 1).astype(BF)
    taps[3 * chan:4 * chan, :] = pltpu.roll(taps[chan:2 * chan, :].astype(F32), wide - 1, 1).astype(BF)

    half = ring * chan

    def pair_copy(q):
        return pltpu.make_async_remote_copy(
            pair_out.at[q], pair_in.at[q], pair_send.at[q], pair_recv.at[q],
            device_id={"ch": sibling}, device_id_type=MESH)

    def relay_copy(q):
        return pltpu.make_async_remote_copy(
            part.at[q, row_far], relay.at[q], relay_send.at[q], relay_recv.at[q],
            device_id={"ch": up if q < PARTS // 2 else down}, device_id_type=MESH)

    def direct_copy(q):
        rising = q >= PARTS // 2
        return pltpu.make_async_remote_copy(
            part.at[q, row_up if rising else row_down], (before if rising else after).at[q],
            direct_send.at[q], direct_recv.at[q],
            device_id={"ch": up if rising else down}, device_id_type=MESH)

    def sum_copy(q):
        rising = q < PARTS // 2
        return pltpu.make_async_remote_copy(
            part.at[q, row_up if rising else row_down], (before if rising else after).at[q],
            sum_send.at[q], sum_recv.at[q],
            device_id={"ch": up if rising else down}, device_id_type=MESH)

    def columns(q):
        return slice(q * piece, (q + 1) * piece)

    def for_sibling(q):
        pair_out[q] = jnp.dot(
            wt[pl.ds(pl.multiple_of((1 - core) * half, half), half), :], taps[:, columns(q)], preferred_element_type=F32
        ).astype(BF).reshape(ring, chan, piece)
        pair_copy(q).start()

    def for_ring(q):
        mine = jnp.dot(
            wt[pl.ds(pl.multiple_of(core * half, half), half), :], taps[:, columns(q)], preferred_element_type=F32)
        pair_copy(q).wait_recv()
        both = mine.reshape(ring, chan, piece) + pair_in[q].astype(F32)
        exact[q] = both
        part[q] = both.astype(BF)
        relay_copy(q).start()

    low = list(range(1, PARTS // 2)) + [0]
    order = [q for both in zip(low, range(PARTS // 2, PARTS)) for q in both]
    for_sibling(order[0])
    for_sibling(order[1])
    for n in range(PARTS):
        for_ring(order[n])
        if n + 2 == PARTS - 2:
            to_up.wait()
            to_down.wait()
            first = halo_odd[...].astype(F32)[:, edge - 1:edge] * jnp.where(me == 0, 0.0, 1.0)
            last = halo_even[...].astype(F32)[:, 0:1] * jnp.where(me == peers - 1, 0.0, 1.0)
            lane = iota((chan, edge), 1)
            taps[0:chan, 0:edge] = jnp.where(lane == 0, first, taps[0:chan, 0:edge].astype(F32)).astype(BF)
            taps[3 * chan:4 * chan, wide - edge:wide] = jnp.where(
                lane == edge - 1, last, taps[3 * chan:4 * chan, wide - edge:wide].astype(F32)).astype(BF)
        if n + 2 < PARTS:
            for_sibling(order[n + 2])
    for q in order:
        direct_copy(q).start()

    load_coarse.wait()
    for source in (sibling, lax.rem(sibling + 2, 2 * ring), lax.rem(sibling + 4, 2 * ring), lax.rem(sibling + 6, 2 * ring)):
        shared(source).wait_recv()
    quarter = wide // 4
    for q in range(4):
        span = slice(q * quarter, (q + 1) * quarter)
        term = lax.dot_general(full[:, span], taps[:, span], NT, preferred_element_type=F32)
        if q == 0:
            weight_acc[...] = term
        else:
            weight_acc[...] += term
    group_rows = channels // outer
    for x in range(outer):
        first_out[x] = weight_acc[x * group_rows:(x + 1) * group_rows, :].astype(BF)

    def first_copy(off):
        other = lax.rem(mine_out + off, outer)
        return pltpu.make_async_remote_copy(
            first_out.at[other], first_in.at[mine_out], first_send.at[other], first_recv.at[mine_out],
            device_id={"pos": other * inner + mine_in}, device_id_type=MESH)

    def first_arrival(off):
        source = lax.rem(mine_out + off, outer)
        return pltpu.make_async_remote_copy(
            first_out.at[source], first_in.at[source], first_send.at[source], first_recv.at[source],
            device_id={"pos": source * inner + mine_in}, device_id_type=MESH), source

    def second_copy(off):
        other = lax.rem(mine_in + off, inner)
        return pltpu.make_async_remote_copy(
            second_out.at[other], second_in.at[mine_in], second_send.at[other], second_recv.at[mine_in],
            device_id={"pos": mine_out * inner + other}, device_id_type=MESH)

    def second_arrival(off):
        source = lax.rem(mine_in + off, inner)
        return pltpu.make_async_remote_copy(
            second_out.at[source], second_in.at[source], second_send.at[source], second_recv.at[source],
            device_id={"pos": mine_out * inner + source}, device_id_type=MESH), source

    for off in range(1, outer):
        first_copy(off).start()

    def pass_on(q):
        rising = q < PARTS // 2
        relay_copy(q).wait_recv()
        to = row_up if rising else row_down
        part[q, to] = (exact[q, to] + relay[q].astype(F32)).astype(BF)
        sum_copy(q).start()

    def drain(off):
        other = lax.rem(me + off, peers)
        for kind in range(3):
            send(kind, other).wait_send()

    each(1, drain)

    for q in order[:PARTS // 2]:
        pass_on(q)

    partial = weight_acc[pl.ds(pl.multiple_of(mine_out * group_rows, group_rows), group_rows), :]
    for off in range(1, outer):
        came, source = first_arrival(off)
        came.wait_recv()
        partial = partial + first_in[source].astype(F32)
    for z in range(inner):
        second_out[z] = partial[z * rows_each:(z + 1) * rows_each]
    for off in range(1, inner):
        second_copy(off).start()

    for q in order[PARTS // 2:]:
        pass_on(q)

    for n, to in enumerate((up, down, far, sibling)):
        share(n, ch, to).wait_send()
    for n, source in enumerate((up, down, far)):
        share(4 + n, source, sibling).wait_send()
    store_skip.wait()
    for q in order:
        pair_copy(q).wait_send()
        relay_copy(q).wait_send()
    for off in range(1, outer):
        first_copy(off).wait_send()

    done = second_out[mine_in]
    for off in range(1, inner):
        came, source = second_arrival(off)
        came.wait_recv()
        done = done + second_in[source]
    done = done * (1.0 / math.sqrt(total))
    for k in range(KERNEL):
        weight_ref[k] = done[:, k * chan:(k + 1) * chan].astype(BF)

    def store(q):
        return pltpu.make_async_copy(coarse_ref.at[:, columns(q)], out_hbm.at[:, columns(q)], store_sem.at[1 + q])

    for q in order:
        direct_copy(q).wait_recv()
        sum_copy(q).wait_recv()
        coarse_ref[:, columns(q)] = (exact[q, row] + before[q].astype(F32) + after[q].astype(F32)).astype(BF)
        store(q).start()

    for q in order:
        direct_copy(q).wait_send()
        sum_copy(q).wait_send()
        store(q).wait()
    for off in range(1, inner):
        second_copy(off).wait_send()


def section(track_grad, activation, coarse_in, tap_weight, score_grad, donor_row, owner, acceptor_row, peers, ring):
    chan, length = activation.shape
    wide = coarse_in.shape[1]
    channels = tap_weight.shape[2]
    count = owner.shape[1]
    cap = count // 8
    fold = length // FOLD
    piece = wide // PARTS
    inner = min(8, peers // 2)
    outer = peers // inner
    outs = KERNEL * chan
    rows_each = channels // peers
    edge = min(128, wide)
    dma = pltpu.SemaphoreType.DMA
    vmem = pl.BlockSpec(memory_space=pltpu.VMEM)
    hbm = pl.BlockSpec(memory_space=pl.ANY)
    slots = pltpu.VMEM((peers, chan, cap), BF)
    names = pltpu.VMEM((peers, 1, cap), jnp.int32)
    quarter = pltpu.VMEM((PARTS, ring, chan, piece), BF)
    eighth = pltpu.VMEM((PARTS, chan, piece), BF)
    return pl.pallas_call(
        functools.partial(section_kernel, peers, inner, ring, wide * peers),
        out_shape=(
            jax.ShapeDtypeStruct((chan, length), BF),
            jax.ShapeDtypeStruct((chan, wide), BF),
            jax.ShapeDtypeStruct((KERNEL, rows_each, chan), BF),
        ),
        in_specs=[hbm, hbm, hbm, vmem, vmem, vmem, vmem, vmem],
        out_specs=(hbm, hbm, vmem),
        scratch_shapes=[
            pltpu.VMEM((chan, length), BF),
            pltpu.VMEM((chan, wide), BF),
            pltpu.VMEM((FOLD * chan, fold), BF),
            pltpu.VMEM((FOLD * chan, fold), BF),
            pltpu.VMEM((FOLD * chan, fold), F32),
            pltpu.VMEM((cap, count), BF),
            pltpu.VMEM((chan, count), BF),
            pltpu.VMEM((GROUP * chan, count), BF),
            pltpu.VMEM((FOLD * chan, BATCH * cap), BF),
            pltpu.VMEM((chan, count), F32),
            names, names, slots, slots, slots, slots,
            pltpu.VMEM((channels, wide), BF),
            pltpu.VMEM((channels, outs), BF),
            pltpu.VMEM((outs, wide), BF),
            pltpu.VMEM((chan, edge), BF),
            pltpu.VMEM((chan, edge), BF),
            quarter, quarter, quarter,
            pltpu.VMEM((PARTS, ring, chan, piece), F32),
            eighth, eighth, eighth,
            pltpu.VMEM((channels, outs), F32),
            pltpu.VMEM((outer, channels // outer, outs), BF),
            pltpu.VMEM((outer, channels // outer, outs), BF),
            pltpu.VMEM((inner, rows_each, outs), F32),
            pltpu.VMEM((inner, rows_each, outs), F32),
            dma((3, FOLD)),
            dma((peers,)), dma((peers,)), dma((peers,)), dma((peers,)), dma((peers,)), dma((peers,)),
            dma((7,)), dma((2 * ring,)), dma((2,)), dma((2,)),
            dma((PARTS,)), dma((PARTS,)), dma((PARTS,)), dma((PARTS,)),
            dma((PARTS,)), dma((PARTS,)), dma((PARTS,)), dma((PARTS,)),
            dma((outer,)), dma((outer,)), dma((inner,)), dma((inner,)), dma((1 + PARTS,)),
        ],
        compiler_params=pltpu.CompilerParams(
            collective_id=1, has_side_effects=True, vmem_limit_bytes=60 * 1024 * 1024),
        name="section",
    )(activation, track_grad, coarse_in, tap_weight, owner, acceptor_row, donor_row, score_grad)


def deliver_kernel(skip_in, coarse_in, weight_in, skip_out, coarse_out, weight_out, skip, coarse, weight, sem):
    parts = 6
    rows = skip.shape[0] // parts
    moves = [(weight_in, weight, weight_out)]
    for n in range(parts):
        span = pl.ds(n * rows, rows)
        for source, held, goal in ((skip_in, skip, skip_out), (coarse_in, coarse, coarse_out)):
            moves.append((source.at[span, :], held.at[span, :], goal.at[span, :]))
    into = [pltpu.make_async_copy(a, b, sem.at[0, n]) for n, (a, b, _) in enumerate(moves)]
    out = [pltpu.make_async_copy(b, c, sem.at[1, n]) for n, (_, b, c) in enumerate(moves)]
    for copy in into:
        copy.start()
    for first, second in zip(into, out):
        first.wait()
        second.start()
    for copy in out:
        copy.wait()


def deliver(*arrays):
    hbm = pl.BlockSpec(memory_space=pl.ANY)
    return pl.pallas_call(
        deliver_kernel,
        out_shape=tuple(jax.ShapeDtypeStruct(a.shape, a.dtype) for a in arrays),
        in_specs=[hbm] * 3,
        out_specs=(hbm,) * 3,
        scratch_shapes=[pltpu.VMEM(a.shape, a.dtype) for a in arrays] + [pltpu.SemaphoreType.DMA((2, 13))],
        name="deliver",
    )(*arrays)


def shards(
    track_grad,
    activation,
    coarse_in,
    tap_weight,
    score_grad,
    donor_row,
    acceptor_owner,
    acceptor_row,
):
    skip_grad, coarse_grad, weight_grad = section(
        track_grad,
        activation,
        coarse_in,
        tap_weight,
        score_grad.reshape(1, -1),
        donor_row.reshape(1, -1),
        acceptor_owner.reshape(1, -1),
        acceptor_row.reshape(1, -1),
        lax.axis_size("pos"),
        lax.axis_size("ch") // 2,
    )
    skip_grad, coarse_grad, weight_grad = deliver(skip_grad, coarse_grad, weight_grad)
    return (skip_grad, coarse_grad, weight_grad.transpose(0, 2, 1))


def solution(mesh):
    in_specs = (
        P("ch", "pos"),
        P("ch", "pos"),
        P("ch", "pos"),
        P(None, "ch", None),
        P("pos"),
        P("pos"),
        P("pos", None),
        P("pos"),
    )
    out_specs = (P("ch", "pos"), P("ch", "pos"), P(None, "ch", "pos"))
    return jax.shard_map(shards, mesh=mesh, in_specs=in_specs, out_specs=out_specs, check_vma=False)
```

```python
import functools
import math

import jax
import jax.numpy as jnp
from jax import lax
from jax.experimental import pallas as pl
from jax.experimental.pallas import tpu as pltpu
from jax.sharding import PartitionSpec as P

C = 768
KERNEL = 4
FOLD = 8
PARTS = 8
GROUP = 8
BATCH = 4
BF = jnp.bfloat16
F32 = jnp.float32
MESH = pl.DeviceIdType.MESH
NT = (((1,), (1,)), ((), ()))


def hot(mask):
    return jnp.where(mask, 1.0, 0.0).astype(BF)


def iota(shape, dim):
    return lax.broadcasted_iota(jnp.int32, shape, dim)


def section_kernel(
    peers, inner, ring, total,
    act_hbm, track_hbm, coarse_hbm, weight_in_ref, owner_ref, acceptor_ref, donor_ref, score_ref,
    skip_hbm, out_hbm, weight_ref,
    skip_ref, coarse_ref, act, track, acc, within_hot, terms, stack, spread, back,
    rows_out, rows_in, terms_out, terms_in, fetch_out, fetch_in,
    full, wt, taps, halo_even, halo_odd, pair_out, pair_in, part, exact, relay, before, after,
    weight_acc, first_out, first_in, second_out, second_in,
    load_sem, rows_send, rows_recv, terms_send, terms_recv, fetch_send, fetch_recv,
    gather_send, gather_recv, halo_send, halo_recv, pair_send, pair_recv, relay_send, relay_recv,
    direct_send, direct_recv, sum_send, sum_recv, first_send, first_recv, second_send, second_recv, store_sem,
):
    me = lax.axis_index("pos")
    ch = lax.axis_index("ch")
    outer = peers // inner
    mine_out, mine_in = me // inner, lax.rem(me, inner)
    core, row = lax.rem(ch, 2), ch // 2
    sibling = ch + 1 - 2 * core
    up = lax.rem(ch + 2, 2 * ring)
    down = lax.rem(ch + 2 * ring - 2, 2 * ring)
    far = lax.rem(ch + 4, 2 * ring)
    row_up, row_down = lax.rem(row + 1, ring), lax.rem(row + ring - 1, ring)
    row_far = lax.rem(row + 2, ring)
    chan, wide = coarse_ref.shape
    piece = wide // PARTS
    count = owner_ref.shape[1]
    cap = within_hot.shape[0]
    fold = act.shape[1]
    per = fold.bit_length() - 1
    channels = full.shape[0]
    rows_each = channels // peers

    def load(which, hbm, ref, g):
        return pltpu.make_async_copy(
            hbm.at[:, pl.ds(g * fold, fold)], ref.at[pl.ds(g * chan, chan), :], load_sem.at[which, g])

    for g in range(FOLD):
        load(0, act_hbm, act, g).start()
    for g in range(FOLD):
        load(1, track_hbm, track, g).start()
    own_rows = pl.ds(pl.multiple_of(ch * chan, chan), chan)
    load_coarse = pltpu.make_async_copy(coarse_hbm, full.at[own_rows, :], load_sem.at[2, 0])
    load_coarse.start()

    def each(first, body):
        def run(off, carry):
            body(off)
            return carry
        lax.fori_loop(first, peers, run, 0)

    barrier = pltpu.get_barrier_semaphore()
    each(1, lambda off: pl.semaphore_signal(
        barrier, inc=1, device_id={"pos": lax.rem(me + off, peers)}, device_id_type=MESH))
    for other in (sibling, up, down, far):
        pl.semaphore_signal(barrier, inc=1, device_id={"ch": other}, device_id_type=MESH)

    owner = owner_ref[...]
    named = jnp.where(owner == iota((peers, count), 0), 1.0, 0.0)
    blocks = count // cap
    stacked = jnp.concatenate([named[:, b * cap:(b + 1) * cap] for b in range(blocks)], axis=0)
    ranks = jnp.dot(stacked.astype(BF), hot(iota((cap, cap), 0) < iota((cap, cap), 1)), preferred_element_type=F32)
    sums = jnp.sum(stacked, axis=1, keepdims=True)
    carried = jnp.zeros((peers, 1), F32)
    for b in range(blocks):
        at = slice(b * peers, (b + 1) * peers)
        within = jnp.sum(stacked[at] * (ranks[at] + carried), axis=0, keepdims=True).astype(jnp.int32)
        within_hot[:, b * cap:(b + 1) * cap] = hot(iota((cap, cap), 0) == within)
        carried = carried + sums[at]
    wanted = acceptor_ref[...]
    planes = jnp.concatenate(
        [named * (wanted >> 7).astype(F32), named * (wanted & 127).astype(F32)], axis=0).astype(BF)
    slots = lax.dot_general(planes, within_hot[...], NT, preferred_element_type=F32)
    rows = (slots[0:peers] * 128.0 + slots[peers:2 * peers]).astype(jnp.int32)
    for p in range(peers):
        rows_out[p] = rows[p:p + 1, :]
    rows_in[me] = rows_out[me]

    def gather(where):
        spot = iota((fold, where.shape[1]), 0)
        prod = jnp.dot(act[...], hot(spot == (where & (fold - 1))), preferred_element_type=F32)
        high = where >> per
        kept = jnp.where(high == 0, prod[0:chan], 0.0)
        for g in range(1, FOLD):
            kept = kept + jnp.where(high == g, prod[g * chan:(g + 1) * chan], 0.0)
        return kept

    for g in range(FOLD):
        load(0, act_hbm, act, g).wait()

    def make_terms(b, carry):
        at = pl.ds(pl.multiple_of(b * BATCH * cap, BATCH * cap), BATCH * cap)
        factor = score_ref[:, at] * (1.0 / math.sqrt(C))
        terms[:, at] = (gather(donor_ref[:, at]) * factor).astype(BF)
        return carry

    lax.fori_loop(0, blocks // BATCH, make_terms, 0)

    def expand(group):
        for k in range(GROUP):
            other = lax.rem(me + group * GROUP + k, peers)
            stack[k * chan:(k + 1) * chan, :] = terms[...] * hot(owner_ref[...] == other)
        slotted = lax.dot_general(stack[...], within_hot[...], NT, preferred_element_type=F32)
        for k in range(GROUP):
            other = lax.rem(me + group * GROUP + k, peers)
            terms_out[other] = slotted[k * chan:(k + 1) * chan, :].astype(BF)

    def leave(group, first):
        for k in range(first, GROUP):
            send(1, lax.rem(me + group * GROUP + k, peers)).start()

    def expand_next(group, carry):
        expand(group)
        leave(group, 0)
        return carry

    pl.semaphore_wait(barrier, peers + 3)

    kinds = (
        (rows_out, rows_in, rows_send, rows_recv),
        (terms_out, terms_in, terms_send, terms_recv),
        (fetch_out, fetch_in, fetch_send, fetch_recv),
    )

    def send(kind, other):
        out, into, sent, got = kinds[kind]
        return pltpu.make_async_remote_copy(
            out.at[other], into.at[me], sent.at[other], got.at[me],
            device_id={"pos": other}, device_id_type=MESH)

    def arrival(kind, other):
        out, into, sent, got = kinds[kind]
        return pltpu.make_async_remote_copy(
            out.at[other], into.at[other], sent.at[other], got.at[other],
            device_id={"pos": other}, device_id_type=MESH)

    each(1, lambda off: send(0, lax.rem(me + off, peers)).start())
    expand(0)
    leave(0, 1)
    terms_in[me] = terms_out[me]

    def share(n, source, goal):
        span = pl.ds(pl.multiple_of(source * chan, chan), chan)
        return pltpu.make_async_remote_copy(
            coarse_hbm if n < 4 else full.at[span, :], full.at[span, :], gather_send.at[n], gather_recv.at[source],
            device_id={"ch": goal}, device_id_type=MESH)

    for n, goal in enumerate((up, down, far, sibling)):
        share(n, ch, goal).start()

    def shared(source):
        span = pl.ds(pl.multiple_of(source * chan, chan), chan)
        return pltpu.make_async_remote_copy(
            full.at[span, :], full.at[span, :], gather_send.at[0], gather_recv.at[source],
            device_id={"ch": sibling}, device_id_type=MESH)

    def look_up(first, second):
        found = gather(jnp.concatenate([rows_in[first], rows_in[second]], axis=1)).astype(BF)
        return found[:, :cap], found[:, cap:]

    def answer(turn, carry):
        first, second = lax.rem(me + 2 * turn + 1, peers), lax.rem(me + 2 * turn + 2, peers)
        arrival(0, first).wait_recv()
        arrival(0, second).wait_recv()
        fetch_out[first], fetch_out[second] = look_up(first, second)
        send(2, first).start()
        send(2, second).start()
        return carry

    lax.fori_loop(0, peers // 2 - 1, answer, 0)
    final = lax.rem(me + peers - 1, peers)
    arrival(0, final).wait_recv()
    fetch_out[final], fetch_in[me] = look_up(final, me)
    send(2, final).start()
    lax.fori_loop(1, peers // GROUP, expand_next, 0)

    for g in range(FOLD):
        load(1, track_hbm, track, g).wait()
    acc[...] = track[...].astype(F32)
    for k in range(KERNEL):
        turned = weight_in_ref[k].astype(F32).T.astype(BF)
        for r in range(ring):
            for c in range(2):
                wt[(c * ring + r) * chan:(c * ring + r + 1) * chan, k * chan:(k + 1) * chan] = (
                    turned[(2 * r + c) * chan:(2 * r + c + 1) * chan])
    back[...] = jnp.zeros_like(back)

    step = min(256, fold)

    def scatter(values, where):
        n = where.shape[1]
        high, low = where >> per, where & (fold - 1)
        for g in range(FOLD):
            spread[g * chan:(g + 1) * chan, 0:n] = values * hot(high == g)
        for r in range(fold // step):
            here = hot(iota((step, n), 0) + r * step == low)
            acc[:, r * step:(r + 1) * step] += lax.dot_general(
                spread[:, 0:n], here, NT, preferred_element_type=F32)

    width = BATCH * cap

    def add_terms(start, size):
        values, where = [], []
        for k in range(size):
            other = lax.rem(me + 2 * peers - (start + k), peers)

            @pl.when(other != me)
            def _():
                arrival(1, other).wait_recv()
            values.append(terms_in[other])
            where.append(rows_in[other])
        scatter(jnp.concatenate(values, axis=1), jnp.concatenate(where, axis=1))

    def add_batch(group, carry):
        add_terms(group * BATCH, BATCH)
        return carry

    lax.fori_loop(0, GROUP // BATCH, add_batch, 0)

    def collect(group, carry):
        held, names = [], []
        for k in range(GROUP):
            other = lax.rem(me + peers - (group * GROUP + k), peers)

            @pl.when(other != me)
            def _():
                arrival(2, other).wait_recv()
            held.append(fetch_in[other])
            names.append(other)
        block = jnp.concatenate(held, axis=0)
        for b in range(blocks):
            at = slice(b * cap, (b + 1) * cap)
            prod = jnp.dot(block, within_hot[:, at], preferred_element_type=F32)
            owners = owner_ref[:, at]
            kept = back[:, at]
            for k in range(GROUP):
                kept = kept + jnp.where(owners == names[k], prod[k * chan:(k + 1) * chan], 0.0)
            back[:, at] = kept
        return carry

    lax.fori_loop(0, peers // GROUP, collect, 0)

    for n, source in enumerate((up, down, far)):
        shared(source).wait_recv()
        share(4 + n, source, sibling).start()

    def add_back(b, carry):
        at = pl.ds(pl.multiple_of(b * width, width), width)
        factor = score_ref[:, at] * (1.0 / math.sqrt(C))
        scatter((back[:, at] * factor).astype(BF), donor_ref[:, at])
        return carry

    lax.fori_loop(0, count // width, add_back, 0)

    lax.fori_loop(GROUP // BATCH, peers // BATCH - 1, add_batch, 0)
    add_terms(peers - BATCH, BATCH // 2)
    add_terms(peers - BATCH // 2, BATCH // 2)

    pair = min(256, fold)
    half_pair = pair // 2
    goal = iota((pair, pair), 1)
    pick = hot(iota((pair, pair), 0) == jnp.where(goal < half_pair, 2 * goal, 2 * (goal - half_pair) + 1))
    edge = halo_even.shape[1]
    to_up = pltpu.make_async_remote_copy(
        taps.at[pl.ds(2 * chan, chan), pl.ds(wide - edge, edge)], halo_odd, halo_send.at[0], halo_recv.at[0],
        device_id={"pos": lax.rem(me + 1, peers)}, device_id_type=MESH)
    to_down = pltpu.make_async_remote_copy(
        taps.at[pl.ds(chan, chan), pl.ds(0, edge)], halo_even, halo_send.at[1], halo_recv.at[1],
        device_id={"pos": lax.rem(me + peers - 1, peers)}, device_id_type=MESH)
    last_q = fold // pair - 1
    for q in [0, last_q] + list(range(1, last_q)):
        at = slice(q * pair, (q + 1) * pair)
        skip = acc[:, at].astype(BF)
        split = jnp.dot(skip, pick, preferred_element_type=F32).astype(BF)
        for g in range(FOLD):
            rows_of = slice(g * chan, (g + 1) * chan)
            skip_ref[:, g * fold + q * pair:g * fold + (q + 1) * pair] = skip[rows_of]
            start = (g * fold + q * pair) // 2
            taps[chan:2 * chan, start:start + half_pair] = split[rows_of, :half_pair]
            taps[2 * chan:3 * chan, start:start + half_pair] = split[rows_of, half_pair:]
        if q == last_q:
            to_down.start()
            to_up.start()
    store_skip = pltpu.make_async_copy(skip_ref, skip_hbm, store_sem.at[0])
    store_skip.start()
    taps[0:chan, :] = pltpu.roll(taps[2 * chan:3 * chan, :].astype(F32), 1, 1).astype(BF)
    taps[3 * chan:4 * chan, :] = pltpu.roll(taps[chan:2 * chan, :].astype(F32), wide - 1, 1).astype(BF)

    half = ring * chan

    def pair_copy(q):
        return pltpu.make_async_remote_copy(
            pair_out.at[q], pair_in.at[q], pair_send.at[q], pair_recv.at[q],
            device_id={"ch": sibling}, device_id_type=MESH)

    def relay_copy(q):
        return pltpu.make_async_remote_copy(
            part.at[q, row_far], relay.at[q], relay_send.at[q], relay_recv.at[q],
            device_id={"ch": up if q < PARTS // 2 else down}, device_id_type=MESH)

    def direct_copy(q):
        rising = q >= PARTS // 2
        return pltpu.make_async_remote_copy(
            part.at[q, row_up if rising else row_down], (before if rising else after).at[q],
            direct_send.at[q], direct_recv.at[q],
            device_id={"ch": up if rising else down}, device_id_type=MESH)

    def sum_copy(q):
        rising = q < PARTS // 2
        return pltpu.make_async_remote_copy(
            part.at[q, row_up if rising else row_down], (before if rising else after).at[q],
            sum_send.at[q], sum_recv.at[q],
            device_id={"ch": up if rising else down}, device_id_type=MESH)

    def columns(q):
        return slice(q * piece, (q + 1) * piece)

    def for_sibling(q):
        pair_out[q] = jnp.dot(
            wt[pl.ds(pl.multiple_of((1 - core) * half, half), half), :], taps[:, columns(q)], preferred_element_type=F32
        ).astype(BF).reshape(ring, chan, piece)
        pair_copy(q).start()

    def for_ring(q):
        mine = jnp.dot(
            wt[pl.ds(pl.multiple_of(core * half, half), half), :], taps[:, columns(q)], preferred_element_type=F32)
        pair_copy(q).wait_recv()
        both = mine.reshape(ring, chan, piece) + pair_in[q].astype(F32)
        exact[q] = both
        part[q] = both.astype(BF)
        relay_copy(q).start()

    low = list(range(1, PARTS // 2)) + [0]
    order = [q for both in zip(low, range(PARTS // 2, PARTS)) for q in both]
    for_sibling(order[0])
    for_sibling(order[1])
    for n in range(PARTS):
        for_ring(order[n])
        if n + 2 == PARTS - 2:
            to_up.wait()
            to_down.wait()
            first = halo_odd[...].astype(F32)[:, edge - 1:edge] * jnp.where(me == 0, 0.0, 1.0)
            last = halo_even[...].astype(F32)[:, 0:1] * jnp.where(me == peers - 1, 0.0, 1.0)
            lane = iota((chan, edge), 1)
            taps[0:chan, 0:edge] = jnp.where(lane == 0, first, taps[0:chan, 0:edge].astype(F32)).astype(BF)
            taps[3 * chan:4 * chan, wide - edge:wide] = jnp.where(
                lane == edge - 1, last, taps[3 * chan:4 * chan, wide - edge:wide].astype(F32)).astype(BF)
        if n + 2 < PARTS:
            for_sibling(order[n + 2])
    for q in order:
        direct_copy(q).start()

    load_coarse.wait()
    for source in (sibling, lax.rem(sibling + 2, 2 * ring), lax.rem(sibling + 4, 2 * ring), lax.rem(sibling + 6, 2 * ring)):
        shared(source).wait_recv()
    quarter = wide // 4
    for q in range(4):
        span = slice(q * quarter, (q + 1) * quarter)
        term = lax.dot_general(full[:, span], taps[:, span], NT, preferred_element_type=F32)
        if q == 0:
            weight_acc[...] = term
        else:
            weight_acc[...] += term
    group_rows = channels // outer
    for x in range(outer):
        first_out[x] = weight_acc[x * group_rows:(x + 1) * group_rows, :].astype(BF)

    def first_copy(off):
        other = lax.rem(mine_out + off, outer)
        return pltpu.make_async_remote_copy(
            first_out.at[other], first_in.at[mine_out], first_send.at[other], first_recv.at[mine_out],
            device_id={"pos": other * inner + mine_in}, device_id_type=MESH)

    def first_arrival(off):
        source = lax.rem(mine_out + off, outer)
        return pltpu.make_async_remote_copy(
            first_out.at[source], first_in.at[source], first_send.at[source], first_recv.at[source],
            device_id={"pos": source * inner + mine_in}, device_id_type=MESH), source

    def second_copy(off):
        other = lax.rem(mine_in + off, inner)
        return pltpu.make_async_remote_copy(
            second_out.at[other], second_in.at[mine_in], second_send.at[other], second_recv.at[mine_in],
            device_id={"pos": mine_out * inner + other}, device_id_type=MESH)

    def second_arrival(off):
        source = lax.rem(mine_in + off, inner)
        return pltpu.make_async_remote_copy(
            second_out.at[source], second_in.at[source], second_send.at[source], second_recv.at[source],
            device_id={"pos": mine_out * inner + source}, device_id_type=MESH), source

    for off in range(1, outer):
        first_copy(off).start()

    def pass_on(q):
        rising = q < PARTS // 2
        relay_copy(q).wait_recv()
        to = row_up if rising else row_down
        part[q, to] = (exact[q, to] + relay[q].astype(F32)).astype(BF)
        sum_copy(q).start()

    def drain(off):
        other = lax.rem(me + off, peers)
        for kind in range(3):
            send(kind, other).wait_send()

    each(1, drain)

    for q in order[:PARTS // 2]:
        pass_on(q)

    partial = weight_acc[pl.ds(pl.multiple_of(mine_out * group_rows, group_rows), group_rows), :]
    for off in range(1, outer):
        came, source = first_arrival(off)
        came.wait_recv()
        partial = partial + first_in[source].astype(F32)
    for z in range(inner):
        second_out[z] = partial[z * rows_each:(z + 1) * rows_each]
    for off in range(1, inner):
        second_copy(off).start()

    for q in order[PARTS // 2:]:
        pass_on(q)

    for n, to in enumerate((up, down, far, sibling)):
        share(n, ch, to).wait_send()
    for n, source in enumerate((up, down, far)):
        share(4 + n, source, sibling).wait_send()
    store_skip.wait()
    for q in order:
        pair_copy(q).wait_send()
        relay_copy(q).wait_send()
    for off in range(1, outer):
        first_copy(off).wait_send()

    done = second_out[mine_in]
    for off in range(1, inner):
        came, source = second_arrival(off)
        came.wait_recv()
        done = done + second_in[source]
    done = done * (1.0 / math.sqrt(total))
    for k in range(KERNEL):
        weight_ref[k] = done[:, k * chan:(k + 1) * chan].astype(BF)

    def store(q):
        return pltpu.make_async_copy(coarse_ref.at[:, columns(q)], out_hbm.at[:, columns(q)], store_sem.at[1 + q])

    for q in order:
        direct_copy(q).wait_recv()
        sum_copy(q).wait_recv()
        coarse_ref[:, columns(q)] = (exact[q, row] + before[q].astype(F32) + after[q].astype(F32)).astype(BF)
        store(q).start()

    for q in order:
        direct_copy(q).wait_send()
        sum_copy(q).wait_send()
        store(q).wait()
    for off in range(1, inner):
        second_copy(off).wait_send()


def section(track_grad, activation, coarse_in, tap_weight, score_grad, donor_row, owner, acceptor_row, peers, ring):
    chan, length = activation.shape
    wide = coarse_in.shape[1]
    channels = tap_weight.shape[2]
    count = owner.shape[1]
    cap = count // 8
    fold = length // FOLD
    piece = wide // PARTS
    inner = min(8, peers // 2)
    outer = peers // inner
    outs = KERNEL * chan
    rows_each = channels // peers
    edge = min(128, wide)
    dma = pltpu.SemaphoreType.DMA
    vmem = pl.BlockSpec(memory_space=pltpu.VMEM)
    hbm = pl.BlockSpec(memory_space=pl.ANY)
    slots = pltpu.VMEM((peers, chan, cap), BF)
    names = pltpu.VMEM((peers, 1, cap), jnp.int32)
    quarter = pltpu.VMEM((PARTS, ring, chan, piece), BF)
    eighth = pltpu.VMEM((PARTS, chan, piece), BF)
    return pl.pallas_call(
        functools.partial(section_kernel, peers, inner, ring, wide * peers),
        out_shape=(
            jax.ShapeDtypeStruct((chan, length), BF),
            jax.ShapeDtypeStruct((chan, wide), BF),
            jax.ShapeDtypeStruct((KERNEL, rows_each, chan), BF),
        ),
        in_specs=[hbm, hbm, hbm, vmem, vmem, vmem, vmem, vmem],
        out_specs=(hbm, hbm, vmem),
        scratch_shapes=[
            pltpu.VMEM((chan, length), BF),
            pltpu.VMEM((chan, wide), BF),
            pltpu.VMEM((FOLD * chan, fold), BF),
            pltpu.VMEM((FOLD * chan, fold), BF),
            pltpu.VMEM((FOLD * chan, fold), F32),
            pltpu.VMEM((cap, count), BF),
            pltpu.VMEM((chan, count), BF),
            pltpu.VMEM((GROUP * chan, count), BF),
            pltpu.VMEM((FOLD * chan, BATCH * cap), BF),
            pltpu.VMEM((chan, count), F32),
            names, names, slots, slots, slots, slots,
            pltpu.VMEM((channels, wide), BF),
            pltpu.VMEM((channels, outs), BF),
            pltpu.VMEM((outs, wide), BF),
            pltpu.VMEM((chan, edge), BF),
            pltpu.VMEM((chan, edge), BF),
            quarter, quarter, quarter,
            pltpu.VMEM((PARTS, ring, chan, piece), F32),
            eighth, eighth, eighth,
            pltpu.VMEM((channels, outs), F32),
            pltpu.VMEM((outer, channels // outer, outs), BF),
            pltpu.VMEM((outer, channels // outer, outs), BF),
            pltpu.VMEM((inner, rows_each, outs), F32),
            pltpu.VMEM((inner, rows_each, outs), F32),
            dma((3, FOLD)),
            dma((peers,)), dma((peers,)), dma((peers,)), dma((peers,)), dma((peers,)), dma((peers,)),
            dma((7,)), dma((2 * ring,)), dma((2,)), dma((2,)),
            dma((PARTS,)), dma((PARTS,)), dma((PARTS,)), dma((PARTS,)),
            dma((PARTS,)), dma((PARTS,)), dma((PARTS,)), dma((PARTS,)),
            dma((outer,)), dma((outer,)), dma((inner,)), dma((inner,)), dma((1 + PARTS,)),
        ],
        compiler_params=pltpu.CompilerParams(
            collective_id=1, has_side_effects=True, vmem_limit_bytes=60 * 1024 * 1024),
        name="section",
    )(activation, track_grad, coarse_in, tap_weight, owner, acceptor_row, donor_row, score_grad)


def deliver_kernel(skip_in, coarse_in, weight_in, skip_out, coarse_out, weight_out, skip, coarse, weight, sem):
    parts = 6
    rows = skip.shape[0] // parts
    moves = [(weight_in, weight, weight_out)]
    for n in range(parts):
        span = pl.ds(n * rows, rows)
        for source, held, goal in ((skip_in, skip, skip_out), (coarse_in, coarse, coarse_out)):
            moves.append((source.at[span, :], held.at[span, :], goal.at[span, :]))
    into = [pltpu.make_async_copy(a, b, sem.at[0, n]) for n, (a, b, _) in enumerate(moves)]
    out = [pltpu.make_async_copy(b, c, sem.at[1, n]) for n, (_, b, c) in enumerate(moves)]
    for copy in into:
        copy.start()
    for first, second in zip(into, out):
        first.wait()
        second.start()
    for copy in out:
        copy.wait()


def deliver(*arrays):
    hbm = pl.BlockSpec(memory_space=pl.ANY)
    return pl.pallas_call(
        deliver_kernel,
        out_shape=tuple(jax.ShapeDtypeStruct(a.shape, a.dtype) for a in arrays),
        in_specs=[hbm] * 3,
        out_specs=(hbm,) * 3,
        scratch_shapes=[pltpu.VMEM(a.shape, a.dtype) for a in arrays] + [pltpu.SemaphoreType.DMA((2, 13))],
        name="deliver",
    )(*arrays)


def shards(
    track_grad,
    activation,
    coarse_in,
    tap_weight,
    score_grad,
    donor_row,
    acceptor_owner,
    acceptor_row,
):
    skip_grad, coarse_grad, weight_grad = section(
        track_grad,
        activation,
        coarse_in,
        tap_weight,
        score_grad.reshape(1, -1),
        donor_row.reshape(1, -1),
        acceptor_owner.reshape(1, -1),
        acceptor_row.reshape(1, -1),
        lax.axis_size("pos"),
        lax.axis_size("ch") // 2,
    )
    skip_grad, coarse_grad, weight_grad = deliver(skip_grad, coarse_grad, weight_grad)
    return (skip_grad, coarse_grad, weight_grad.transpose(0, 2, 1))


def solution(mesh):
    in_specs = (
        P("ch", "pos"),
        P("ch", "pos"),
        P("ch", "pos"),
        P(None, "ch", None),
        P("pos"),
        P("pos"),
        P("pos", None),
        P("pos"),
    )
    out_specs = (P("ch", "pos"), P("ch", "pos"), P(None, "ch", "pos"))
    return jax.shard_map(shards, mesh=mesh, in_specs=in_specs, out_specs=out_specs, check_vma=False)
```
